32 devices in a mesh: ctx: 16 (over z, y, core), tp: 2 (over x).
Axes of the slice: x: 2, y: 2, z: 4, core: 2. Of those that a mesh axis runs over, the one named last changes fastest.
Arguments:
- queries: bfloat16 [8192, 8192], P('ctx', 'tp'), may hold values from -132 to 132
- keys: bfloat16 [8192, 1024], P('ctx', 'tp'), may hold values from -6 to 6
- values: bfloat16 [8192, 1024], P('ctx', 'tp'), may hold values from -6 to 6
- prefix_spans: int32 [16], P('ctx'), may hold values from 1 to 7, as said below
Outputs:
- attended: bfloat16 [8192, 8192], P('ctx', 'tp')
The draws below stay inside these ranges and needn't reach their ends.
Inputs may be any that keep to these rules, and one draw needn't show every extreme that they name: `prefix_spans`: 7 is reached by some block in every draw.
All inputs are finite; a program needn't handle non-finite values.
Results may differ from the reference program's by a relative error of at most 0.003.
Values may be sent and summed in bfloat16 or wider, within the bound.
No kernel may reach another device: no remote copies, remote signals or barrier semaphores. Data moves between devices by JAX's collectives and lax.ppermute only.
A program may use at most 384 MiB of HBM per device.

```python
import math
import jax
import jax.numpy as jnp
from jax import lax

QUERY_HEAD_COUNT = 64
KEY_VALUE_HEADS = 8
HEAD_SIZE = 128
BLOCK_LENGTH = 512
PREFIX_BLOCK_MAX = 7
TOKEN_COUNT = 8192


def common_pattern(key):
    key_seed_base = jax.random.fold_in(key, 102)
    random_base_keys = jnp.clip(jax.random.normal(key_seed_base, (TOKEN_COUNT, KEY_VALUE_HEADS, HEAD_SIZE), jnp.float32), -6.0, 6.0)
    return random_base_keys


def draw_keys(key, part):
    random_base_keys = common_pattern(key)
    result_output = random_base_keys
    return result_output.reshape(TOKEN_COUNT, KEY_VALUE_HEADS * HEAD_SIZE).astype(jnp.bfloat16)


def draw_queries(key, part):
    key = jax.random.fold_in(key, 2)
    query_group = QUERY_HEAD_COUNT // KEY_VALUE_HEADS
    result_output = jnp.clip(2.5 * jax.random.normal(key, (TOKEN_COUNT, KEY_VALUE_HEADS, query_group, HEAD_SIZE), jnp.float32), -20.0, 20.0)
    return result_output.reshape(TOKEN_COUNT, QUERY_HEAD_COUNT * HEAD_SIZE).astype(jnp.bfloat16)


def draw_prefix_spans(key, part):
    key = jax.random.fold_in(key, 3)
    block_list = TOKEN_COUNT // BLOCK_LENGTH
    counts = jax.random.randint(key, (block_list,), 1, PREFIX_BLOCK_MAX + 1, jnp.int32)
    pick = jax.random.randint(jax.random.fold_in(key, 4), (), 0, block_list, jnp.int32)
    return counts.at[pick].set(PREFIX_BLOCK_MAX)


def level_of(key, extent, shards, low, high):
    gain = 1.0
    for axis_at, blocks in shards:
        steps = jax.random.uniform(jax.random.fold_in(jax.random.fold_in(key, 6), axis_at), (blocks,), jnp.float32, low / len(shards), high / len(shards))
        gain = gain * jnp.repeat(jnp.exp(steps), extent[axis_at] // blocks).reshape((-1,) + (1,) * (len(extent) - 1 - axis_at))
    return gain


def normal_values(own_key, shape, scale, most, pieces=(), kind=jnp.bfloat16):
    drawn = jax.random.normal(own_key, shape, jnp.float32) * scale
    if len(pieces) > 0:
        drawn = level_of(own_key, shape, pieces, -0.22, 0.18) * drawn
    return jnp.clip(drawn, min=-most, max=most).astype(kind)


def setup_inputs(seed: int = 0) -> dict:
    arg_keys = jax.random.split(jax.random.key(seed), 5)
    return {
        "queries": draw_queries(jax.random.fold_in(arg_keys[4], 71), 0),
        "keys": draw_keys(jax.random.fold_in(arg_keys[4], 71), 0),
        "values": normal_values(arg_keys[2], (TOKEN_COUNT, KEY_VALUE_HEADS * HEAD_SIZE), 1.0, 6.0, ((0, 16), (1, 2))),
        "prefix_spans": draw_prefix_spans(jax.random.fold_in(arg_keys[4], 71), 0),
    }


def block_update(running_state, scores, vals):
    running_max, total, acc = running_state
    new_max = jnp.maximum(running_max, lax.optimization_barrier(jnp.max(scores, axis=-1)))
    correct = jnp.exp(running_max - new_max)
    probs = jnp.exp(scores - new_max[..., None])
    total = total * correct + lax.optimization_barrier(jnp.sum(probs, axis=-1))
    rounded = lax.optimization_barrier(probs.astype(jnp.bfloat16))
    acc = acc * correct[..., None] + jnp.einsum('rhgt,thd->rhgd', rounded.astype(jnp.float32), vals)
    return (new_max, total, acc)

def reference(queries, keys, values, prefix_spans):
    query_group = QUERY_HEAD_COUNT // KEY_VALUE_HEADS
    block_list = TOKEN_COUNT // BLOCK_LENGTH
    scale = 1.0 / math.sqrt(HEAD_SIZE)
    query_head_rows = queries.reshape(block_list, BLOCK_LENGTH, KEY_VALUE_HEADS, query_group, HEAD_SIZE)
    key_head_rows = keys.reshape(block_list, BLOCK_LENGTH, KEY_VALUE_HEADS, HEAD_SIZE)
    value_head_rows = values.reshape(block_list, BLOCK_LENGTH, KEY_VALUE_HEADS, HEAD_SIZE)
    padding_width = jnp.zeros((PREFIX_BLOCK_MAX, BLOCK_LENGTH, KEY_VALUE_HEADS, HEAD_SIZE), jnp.bfloat16)
    key_padded = jnp.concatenate([padding_width, key_head_rows], axis=0)
    value_padded = jnp.concatenate([padding_width, value_head_rows], axis=0)
    row_ids = jnp.arange(BLOCK_LENGTH, dtype=jnp.int32)[:, None, None, None]
    col_ids = jnp.arange(BLOCK_LENGTH, dtype=jnp.int32)[None, None, None, :]

    def one_block(index):
        qf = lax.dynamic_index_in_dim(query_head_rows, index, 0, keepdims=False).astype(jnp.float32)
        limit = lax.dynamic_index_in_dim(prefix_spans, index, 0, keepdims=False)
        running_state = (jnp.full((BLOCK_LENGTH, KEY_VALUE_HEADS, query_group), -jnp.inf, jnp.float32), jnp.zeros((BLOCK_LENGTH, KEY_VALUE_HEADS, query_group), jnp.float32), jnp.zeros((BLOCK_LENGTH, KEY_VALUE_HEADS, query_group, HEAD_SIZE), jnp.float32))
        for step in range(PREFIX_BLOCK_MAX + 1):
            where_at = (index + PREFIX_BLOCK_MAX - step).astype(jnp.int32)
            key_block = lax.dynamic_index_in_dim(key_padded, where_at, 0, keepdims=False).astype(jnp.float32)
            value_block = lax.dynamic_index_in_dim(value_padded, where_at, 0, keepdims=False).astype(jnp.float32)
            scores = jnp.einsum('rhgd,thd->rhgt', qf, key_block) * scale
            if step == 0:
                admitted = row_ids >= col_ids
            else:
                admitted = jnp.logical_and(step <= limit, index - step >= 0)
            scores = jnp.where(admitted, scores, -jnp.inf)
            running_state = block_update(running_state, scores, value_block)
        output = running_state[2] / running_state[1][..., None]
        return output.reshape(BLOCK_LENGTH, QUERY_HEAD_COUNT * HEAD_SIZE).astype(jnp.bfloat16)
    result_output = lax.map(one_block, jnp.arange(block_list, dtype=jnp.int32))
    return result_output.reshape(TOKEN_COUNT, QUERY_HEAD_COUNT * HEAD_SIZE)
```

```python
import functools
import math

import jax
import jax.numpy as jnp
from jax import lax
from jax.experimental import pallas as pl
from jax.experimental.pallas import tpu as pltpu
from jax.sharding import PartitionSpec as P

QUERY_HEAD_COUNT = 64
KEY_VALUE_HEADS = 8
HEAD_SIZE = 128
PREFIX_BLOCK_MAX = 7
GROUP = QUERY_HEAD_COUNT // KEY_VALUE_HEADS
SCALE = math.log2(math.e) / math.sqrt(HEAD_SIZE)
CHUNK = 256


def passed_along(shard, axis, by):
    length = lax.axis_size(axis)
    pairs = [(i, i + by) for i in range(length) if 0 <= i + by < length]
    return lax.ppermute(shard, axis, pairs)


def scores_of(k, q):
    return lax.dot_general(k, q, (((1,), (1,)), ((), ())), preferred_element_type=jnp.float32)


def head_cols(i):
    return pl.ds(pl.multiple_of(i * HEAD_SIZE, HEAD_SIZE), HEAD_SIZE)


def attend_kernel(first, last, *refs):
    if first:
        q_ref, k_ref, v_ref, acc_out, m_out, l_out, s0, s1, vt = refs
        acc_in = m_in = l_in = None
    elif last:
        flag, q_ref, k_ref, v_ref, acc_in, m_in, l_in, out_ref, s0, s1, vt = refs
    else:
        flag, q_ref, k_ref, v_ref, acc_in, m_in, l_in, acc_out, m_out, l_out, s0, s1, vt = refs
    rows = q_ref.shape[0]

    def write(i, acc, m, l):
        if last:
            out_ref[:, head_cols(i)] = (acc / l).T.astype(out_ref.dtype)
        else:
            acc_out[head_cols(i), :] = acc
            m_out[pl.ds(i, 1), :] = m
            l_out[pl.ds(i, 1), :] = l

    def compute_scores(i, s):
        s[...] = scores_of(k_ref[0], q_ref[:, head_cols(i)])

    def update(i, s):
        if first:
            keys_at = lax.broadcasted_iota(jnp.int32, (rows, rows), 0)
            queries_at = lax.broadcasted_iota(jnp.int32, (rows, rows), 1)
            s[...] = jnp.where(queries_at >= keys_at, s[...], -jnp.inf)
        top = jnp.max(s[...], axis=0, keepdims=True) * SCALE
        if first:
            m = top
        else:
            m_old = m_in[pl.ds(i, 1), :]
            m = jnp.maximum(m_old, top)
            correct = jnp.exp2(m_old - m)
        l = None
        acc = None
        for at in range(0, rows, CHUNK):
            p = jnp.exp2(s[at:at + CHUNK, :] * SCALE - m)
            part = jnp.sum(p, axis=0, keepdims=True)
            l = part if l is None else l + part
            o = jnp.dot(vt[:, at:at + CHUNK], p.astype(jnp.bfloat16), preferred_element_type=jnp.float32)
            acc = o if acc is None else acc + o
        if not first:
            l = l_in[pl.ds(i, 1), :] * correct + l
            acc = acc_in[head_cols(i), :] * correct + acc
        write(i, acc, m, l)

    def attend():
        vt[...] = v_ref[0].T
        compute_scores(0, s0)

        def pair(t, carry):
            i = 2 * t
            compute_scores(i + 1, s1)
            update(i, s0)
            compute_scores(jnp.minimum(i + 2, GROUP - 1), s0)
            update(i + 1, s1)
            return carry

        lax.fori_loop(0, GROUP // 2, pair, 0)

    if first:
        attend()
    else:
        admitted = flag[0] != 0
        pl.when(admitted)(attend)

        @pl.when(jnp.logical_not(admitted))
        def _():
            def keep(i, carry):
                write(i, acc_in[head_cols(i), :], m_in[pl.ds(i, 1), :], l_in[pl.ds(i, 1), :])
                return carry

            lax.fori_loop(0, GROUP, keep, 0)


def attend(q, kv, state, flag, last):
    first = state is None
    rows, width = q.shape
    heads = width // HEAD_SIZE
    kv_local = heads // GROUP
    span = GROUP * HEAD_SIZE
    q_spec = pl.BlockSpec((rows, span), lambda h: (0, h))
    in_specs = [
        q_spec,
        pl.BlockSpec((1, rows, HEAD_SIZE), lambda h: (0, 0, h)),
        pl.BlockSpec((1, rows, HEAD_SIZE), lambda h: (1, 0, h)),
    ]
    args = [q, kv, kv]
    acc_spec = pl.BlockSpec((span, rows), lambda h: (h, 0))
    row_spec = pl.BlockSpec((GROUP, rows), lambda h: (h, 0))
    if not first:
        in_specs = [pl.BlockSpec(memory_space=pltpu.SMEM)] + in_specs + [acc_spec, row_spec, row_spec]
        args = [flag] + args + list(state)
    if last:
        out_specs = q_spec
        out_shape = jax.ShapeDtypeStruct(q.shape, q.dtype)
    else:
        out_specs = [acc_spec, row_spec, row_spec]
        out_shape = [
            jax.ShapeDtypeStruct((width, rows), jnp.float32),
            jax.ShapeDtypeStruct((heads, rows), jnp.float32),
            jax.ShapeDtypeStruct((heads, rows), jnp.float32),
        ]
    return pl.pallas_call(
        functools.partial(attend_kernel, first, last),
        grid=(kv_local,),
        in_specs=in_specs,
        out_specs=out_specs,
        out_shape=out_shape,
        scratch_shapes=[
            pltpu.VMEM((rows, rows), jnp.float32),
            pltpu.VMEM((rows, rows), jnp.float32),
            pltpu.VMEM((HEAD_SIZE, rows), jnp.bfloat16),
        ],
        compiler_params=pltpu.CompilerParams(vmem_limit_bytes=48 * 1024 * 1024),
        cost_estimate=pl.CostEstimate(
            flops=4 * heads * rows * rows * HEAD_SIZE,
            bytes_accessed=2 * 4 * width * rows,
            transcendentals=heads * rows * rows,
        ),
        name="attend_diagonal" if first else "attend_block",
    )(*args)


def on_device(queries, keys, values, prefix_spans):
    own = jnp.stack([keys, values])
    position = lax.axis_index("ctx")
    reach = jnp.minimum(prefix_spans, position)
    carried = passed_along(own, "ctx", 1)
    state = attend(queries, own, None, None, False)
    for step in range(1, PREFIX_BLOCK_MAX + 1):
        piece = carried
        if step < PREFIX_BLOCK_MAX:
            carried = passed_along(piece, "ctx", 1)
        flag = (reach >= step).astype(jnp.int32)
        state = attend(queries, piece, state, flag, step == PREFIX_BLOCK_MAX)
    return state


def solution(mesh):
    placed = (P("ctx", "tp"), P("ctx", "tp"), P("ctx", "tp"), P("ctx"))
    return jax.shard_map(
        on_device, mesh=mesh, in_specs=placed, out_specs=P("ctx", "tp"), check_vma=False
    )
```

```python
import functools
import math

import jax
import jax.numpy as jnp
from jax import lax
from jax.experimental import pallas as pl
from jax.experimental.pallas import tpu as pltpu
from jax.sharding import PartitionSpec as P

QUERY_HEAD_COUNT = 64
KEY_VALUE_HEADS = 8
HEAD_SIZE = 128
PREFIX_BLOCK_MAX = 7
GROUP = QUERY_HEAD_COUNT // KEY_VALUE_HEADS
SCALE = math.log2(math.e) / math.sqrt(HEAD_SIZE)
VMEM_LIMIT = 48 * 1024 * 1024


def moved(shard, pairs):
    return lax.ppermute(shard, "ctx", pairs)


def head_rows(i):
    return slice(i * HEAD_SIZE, (i + 1) * HEAD_SIZE)


def column_max(s):
    return jnp.max(s, axis=0, keepdims=True)


def column_sum(s):
    return jnp.sum(s, axis=0, keepdims=True)


def dot(a, b):
    return jnp.dot(a, b, preferred_element_type=jnp.float32)


def attend_block(k_at, v_at, qt_ref, acc_ref, m_ref, l_ref, s_refs, vt_ref):
    heads = m_ref.shape[0]
    rows = qt_ref.shape[1]
    half = rows // 2
    vt_ref[...] = v_at(slice(None)).T

    def scores(i, c):
        s = dot(k_at(slice(c * half, (c + 1) * half)), qt_ref[head_rows(i), :])
        s_refs[i % 2][c * half:(c + 1) * half, :] = s
        return column_max(s)

    top = jnp.maximum(scores(0, 0), scores(0, 1))
    for i in range(heads):
        m_old = m_ref[i:i + 1, :]
        m = jnp.maximum(m_old, top * SCALE)
        correct = jnp.exp2(m_old - m)
        tops, l, acc = [], l_ref[i:i + 1, :] * correct, None
        for c in range(2):
            at = slice(c * half, (c + 1) * half)
            if i + 1 < heads:
                tops.append(scores(i + 1, c))
            p = jnp.exp2(s_refs[i % 2][at, :] * SCALE - m)
            l = l + column_sum(p)
            o = dot(vt_ref[:, at], p.astype(jnp.bfloat16))
            acc = o if acc is None else acc + o
        acc_ref[head_rows(i), :] = acc_ref[head_rows(i), :] * correct + acc
        m_ref[i:i + 1, :] = m
        l_ref[i:i + 1, :] = l
        if tops:
            top = jnp.maximum(tops[0], tops[1])


def attend_diagonal(k_at, v_at, qt_ref, acc_ref, m_ref, l_ref, s_refs, vt_ref):
    heads = m_ref.shape[0]
    rows = qt_ref.shape[1]
    half = rows // 2
    vt_ref[...] = v_at(slice(None)).T
    lower = lax.broadcasted_iota(jnp.int32, (half, half), 0) <= lax.broadcasted_iota(
        jnp.int32, (half, half), 1
    )

    def masked(s):
        return jnp.where(lower, s, -jnp.inf)

    def scores(i):
        s_ref = s_refs[i % 2]
        near = masked(dot(k_at(slice(0, half)), qt_ref[head_rows(i), :half]))
        over = dot(k_at(slice(0, half)), qt_ref[head_rows(i), half:])
        far = masked(dot(k_at(slice(half, rows)), qt_ref[head_rows(i), half:]))
        s_ref[:half, :half] = near
        s_ref[:half, half:] = over
        s_ref[half:, half:] = far
        return column_max(near), jnp.maximum(column_max(over), column_max(far))

    top = scores(0)
    for i in range(heads):
        s_ref = s_refs[i % 2]
        following = scores(i + 1) if i + 1 < heads else None
        m0, m1 = top[0] * SCALE, top[1] * SCALE
        near = jnp.exp2(s_ref[:half, :half] * SCALE - m0)
        over = jnp.exp2(s_ref[:half, half:] * SCALE - m1)
        far = jnp.exp2(s_ref[half:, half:] * SCALE - m1)
        acc_ref[head_rows(i), :half] = dot(vt_ref[:, :half], near.astype(jnp.bfloat16))
        acc_ref[head_rows(i), half:] = dot(vt_ref[:, :half], over.astype(jnp.bfloat16)) + dot(
            vt_ref[:, half:], far.astype(jnp.bfloat16)
        )
        m_ref[i:i + 1, :half] = m0
        m_ref[i:i + 1, half:] = m1
        l_ref[i:i + 1, :half] = column_sum(near)
        l_ref[i:i + 1, half:] = column_sum(over) + column_sum(far)
        top = following


def reader(ref, *lead):
    return lambda at: ref[(*lead, at, slice(None))]


def local_kernel(
    flags, q_own, q_other, k_own, v_own, k_other, v_other,
    qt_ref, acc_ref, m_ref, l_ref, s0, s1, vt,
):
    b = pl.program_id(0)
    heads = m_ref.shape[0]
    state = (qt_ref, acc_ref, m_ref, l_ref, (s0, s1), vt)

    def whole(q_ref, own, other):
        for i in range(heads):
            qt_ref[head_rows(i), :] = q_ref[:, head_rows(i)].T
        attend_diagonal(*own, *state)

        @pl.when(flags[1 + b] > 0)
        def _():
            attend_block(*other, *state)

    mine = (reader(k_own), reader(v_own))
    theirs = (reader(k_other), reader(v_other))
    pl.when(b == 0)(lambda: whole(q_own, mine, theirs))
    pl.when(b == 1)(lambda: whole(q_other, theirs, mine))


def window_kernel(pieces, side, flags, *refs):
    last = side is not None
    qt_ref, kv_refs = refs[0], refs[1:1 + 2 * pieces]
    acc_in, m_in, l_in = refs[1 + 2 * pieces:4 + 2 * pieces]
    rest = refs[4 + 2 * pieces:]
    if last:
        out_ref, acc_ref, m_ref, l_ref, s0, s1, vt = rest
    else:
        acc_ref, m_ref, l_ref, s0, s1, vt = rest
    b = side if last else pl.program_id(0)
    acc_ref[...] = acc_in[...]
    m_ref[...] = m_in[...]
    l_ref[...] = l_in[...]
    for n in range(pieces):
        k_ref, v_ref = kv_refs[2 * n:2 * n + 2]

        def step(t, carry, k_ref=k_ref, v_ref=v_ref):
            slot = jnp.where(flags[0] == 0, 1 - t, t)
            attend_block(
                reader(k_ref, slot), reader(v_ref, slot), qt_ref, acc_ref, m_ref, l_ref, (s0, s1), vt
            )
            return carry

        lax.fori_loop(0, flags[1 + 2 * n + b], step, 0)
    if last:
        for i in range(m_ref.shape[0]):
            out = acc_ref[head_rows(i), :] / l_ref[i:i + 1, :]
            out_ref[:, head_rows(i)] = out.T.astype(out_ref.dtype)


def scratch(rows):
    return [
        pltpu.VMEM((rows, rows), jnp.float32),
        pltpu.VMEM((rows, rows), jnp.float32),
        pltpu.VMEM((HEAD_SIZE, rows), jnp.bfloat16),
    ]


def cost(heads, rows, blocks):
    return pl.CostEstimate(
        flops=int(4 * heads * rows * rows * HEAD_SIZE * blocks),
        bytes_accessed=2 * 4 * heads * HEAD_SIZE * rows,
        transcendentals=int(heads * rows * rows * blocks),
    )


def state_specs(group, rows, kv_heads):
    span = group * HEAD_SIZE
    at = lambda b, h, flags: (b * kv_heads + h, 0)
    return (
        pl.BlockSpec((span, rows), at),
        pl.BlockSpec((None, group, rows), lambda b, h, flags: (b * kv_heads + h, 0, 0)),
    )


def local_attention(flags, queries, own_kv, received, group, kv_heads):
    rows = queries.shape[0]
    span = group * HEAD_SIZE
    units = 2 * kv_heads
    q_tiles = kv_heads * group
    wide, thin = state_specs(group, rows, kv_heads)
    column = lambda width, index: pl.BlockSpec((rows, width), index)
    grid_spec = pltpu.PrefetchScalarGridSpec(
        num_scalar_prefetch=1,
        grid=(2, kv_heads),
        in_specs=[
            column(span, lambda b, h, flags: (0, flags[0] * kv_heads + jnp.where(b == 0, h, kv_heads - 1))),
            column(span, lambda b, h, flags: (0, jnp.where(b == 0, 0, h))),
            column(HEAD_SIZE, lambda b, h, flags: (0, h)),
            column(HEAD_SIZE, lambda b, h, flags: (0, kv_heads + h)),
            column(HEAD_SIZE, lambda b, h, flags: (0, q_tiles + h)),
            column(HEAD_SIZE, lambda b, h, flags: (0, q_tiles + kv_heads + h)),
        ],
        out_specs=[wide, wide, thin, thin],
        scratch_shapes=scratch(rows),
    )
    stats = jax.ShapeDtypeStruct((units, group, rows), jnp.float32)
    return pl.pallas_call(
        local_kernel,
        grid_spec=grid_spec,
        out_shape=[
            jax.ShapeDtypeStruct((units * span, rows), jnp.bfloat16),
            jax.ShapeDtypeStruct((units * span, rows), jnp.float32),
            stats,
            stats,
        ],
        compiler_params=pltpu.CompilerParams(vmem_limit_bytes=VMEM_LIMIT),
        cost_estimate=cost(units * group, rows, 1),
        name="attend_local",
    )(flags, queries, received, own_kv, own_kv, received, received)


def window_attention(flags, qt, pairs, state, group, kv_heads, name):
    rows = qt.shape[1]
    units = 2 * kv_heads
    wide, thin = state_specs(group, rows, kv_heads)
    kv_specs, kv_args = [], []
    for pair in pairs:
        for offset in (0, kv_heads):
            kv_specs.append(
                pl.BlockSpec((2, rows, HEAD_SIZE), lambda b, h, flags, offset=offset: (0, 0, offset + h))
            )
            kv_args.append(pair)
    grid_spec = pltpu.PrefetchScalarGridSpec(
        num_scalar_prefetch=1,
        grid=(2, kv_heads),
        in_specs=[wide, *kv_specs, wide, thin, thin],
        out_specs=[wide, thin, thin],
        scratch_shapes=scratch(rows),
    )
    return pl.pallas_call(
        functools.partial(window_kernel, len(pairs), None),
        grid_spec=grid_spec,
        out_shape=[jax.ShapeDtypeStruct(a.shape, a.dtype) for a in state],
        compiler_params=pltpu.CompilerParams(vmem_limit_bytes=VMEM_LIMIT),
        cost_estimate=cost(units * group, rows, 2 * len(pairs)),
        name=name,
    )(flags, qt, *kv_args, *state)


def last_attention(flags, qt, pair, state, group, kv_heads, side, width, name):
    rows = qt.shape[1]
    span = group * HEAD_SIZE
    first = side * kv_heads
    wide = pl.BlockSpec((span, rows), lambda b, h, flags: (first + h, 0))
    thin = pl.BlockSpec((None, group, rows), lambda b, h, flags: (first + h, 0, 0))
    kv_specs = [
        pl.BlockSpec((2, rows, HEAD_SIZE), lambda b, h, flags, offset=offset: (0, 0, offset + h))
        for offset in (0, kv_heads)
    ]
    if side == 0:
        out_at = lambda b, h, flags: (0, flags[0] * kv_heads + h)
    else:
        out_at = lambda b, h, flags: (0, h)
    grid_spec = pltpu.PrefetchScalarGridSpec(
        num_scalar_prefetch=1,
        grid=(1, kv_heads),
        in_specs=[wide, *kv_specs, wide, thin, thin],
        out_specs=pl.BlockSpec((rows, span), out_at),
        scratch_shapes=[
            pltpu.VMEM((span, rows), jnp.float32),
            pltpu.VMEM((group, rows), jnp.float32),
            pltpu.VMEM((group, rows), jnp.float32),
            *scratch(rows),
        ],
    )
    return pl.pallas_call(
        functools.partial(window_kernel, 1, side),
        grid_spec=grid_spec,
        out_shape=jax.ShapeDtypeStruct((rows, width), jnp.bfloat16),
        compiler_params=pltpu.CompilerParams(vmem_limit_bytes=VMEM_LIMIT),
        cost_estimate=cost(kv_heads * group, rows, 2),
        name=name,
    )(flags, qt, pair, pair, *state)


def on_device(queries, keys, values, prefix_spans):
    rows, width = queries.shape
    length = lax.axis_size("ctx")
    kv_local = keys.shape[1] // HEAD_SIZE
    if kv_local % 2 == 0:
        kv_heads, group = kv_local // 2, GROUP
    else:
        kv_heads, group = kv_local, GROUP // 2
    q_width, kv_width = width // 2, kv_heads * HEAD_SIZE

    position = lax.axis_index("ctx")
    core = position % 2
    upper = (position // 2) % 2
    swap = [(i, i ^ 1) for i in range(length)]
    across = [(i, i ^ 2) for i in range(length)]
    ahead = [(i, i + 4) for i in range(length - 4)]
    climb = [(i, i + 2) for i in range(length) if i % 4 < 2]
    ahead_lower = [(i, i + 4) for i in range(length - 4) if i % 4 < 2]

    def heads_of(side):
        if kv_local % 2 == 0:
            cut = lambda a: lax.dynamic_slice_in_dim(a, side * kv_width, kv_width, 1)
            return jnp.concatenate([cut(keys), cut(values)], axis=1)
        return jnp.concatenate([keys, values], axis=1)

    q_other = lax.dynamic_slice_in_dim(queries, (1 - core) * q_width, q_width, 1)
    span_columns = jnp.broadcast_to(prefix_spans.astype(jnp.bfloat16), (rows, HEAD_SIZE))
    received = moved(jnp.concatenate([q_other, heads_of(1 - core), span_columns], axis=1), swap)
    own_kv = heads_of(core)
    pair = jnp.stack([own_kv, received[:, q_width:q_width + 2 * kv_width]])

    reach_own = jnp.minimum(prefix_spans[0], position)
    other_span = received[0, q_width + 2 * kv_width].astype(jnp.int32)
    reach_other = jnp.minimum(other_span, position ^ 1)
    odd_own = core
    odd_other = 1 - core

    def count(distance, there):
        first = 2 * distance - 1
        own = jnp.clip(reach_own - (first + odd_own) + 1, 0, 2)
        other = jnp.clip(reach_other - (first + odd_other) + 1, 0, 2)
        return [jnp.where(there, own, 0), jnp.where(there, other, 0)]

    def flags_of(*counts):
        return jnp.stack([core, *[n for pair_counts in counts for n in pair_counts]]).astype(jnp.int32)

    always = position >= 0
    is_upper = upper == 1
    is_lower = upper == 0
    select = lambda a, b: [jnp.where(is_lower, x, y) for x, y in zip(a, b)]

    near = moved(pair, ahead)
    below = moved(pair, climb)

    local_flags = jnp.stack(
        [core, jnp.logical_and(odd_own == 1, reach_own >= 1), jnp.logical_and(odd_other == 1, reach_other >= 1)]
    ).astype(jnp.int32)
    qt, *state = local_attention(local_flags, queries, own_kv, received, group, kv_heads)

    near, below, *state = lax.optimization_barrier((near, below, *state))
    beside = moved(near, across)
    far = moved(near, ahead)
    flags = flags_of(count(2, always), count(1, is_upper))
    state = window_attention(flags, qt, (near, below), state, group, kv_heads, "attend_near")

    beside, far, *state = lax.optimization_barrier((beside, far, *state))
    third = moved(beside, ahead_lower)
    flags = flags_of(select(count(1, always), count(3, always)), count(4, always))
    state = window_attention(flags, qt, (beside, far), state, group, kv_heads, "attend_beside")

    third, *state = lax.optimization_barrier((third, *state))
    flags = flags_of(count(3, is_lower))
    for_other = last_attention(flags, qt, third, state, group, kv_heads, 1, q_width, "attend_last_other")
    returned = moved(for_other, swap)
    out = last_attention(flags, qt, third, state, group, kv_heads, 0, width, "attend_last_own")
    return lax.dynamic_update_slice_in_dim(out, returned, (1 - core) * q_width, 1)


def solution(mesh):
    placed = (P("ctx", "tp"), P("ctx", "tp"), P("ctx", "tp"), P("ctx"))
    return jax.shard_map(
        on_device, mesh=mesh, in_specs=placed, out_specs=P("ctx", "tp"), check_vma=False
    )
```

```python
import functools
import math

import jax
import jax.numpy as jnp
from jax import lax
from jax.experimental import pallas as pl
from jax.experimental.pallas import tpu as pltpu
from jax.sharding import PartitionSpec as P

QUERY_HEAD_COUNT = 64
KEY_VALUE_HEADS = 8
HEAD_SIZE = 128
GROUP = QUERY_HEAD_COUNT // KEY_VALUE_HEADS
SCALE = math.log2(math.e) / math.sqrt(HEAD_SIZE)
VMEM_LIMIT = 28 * 1024 * 1024


def moved(shard, pairs):
    return lax.ppermute(shard, "ctx", pairs)


def head_rows(i):
    return slice(i * HEAD_SIZE, (i + 1) * HEAD_SIZE)


def column_max(s):
    return jnp.max(s, axis=0, keepdims=True)


def column_sum(s):
    return jnp.sum(s, axis=0, keepdims=True)


def dot(a, b):
    return jnp.dot(a, b, preferred_element_type=jnp.float32)


class Step:
    def __init__(self, refs, kv_ref, slot, head, at):
        self.qt_ref, self.acc_ref, self.m_ref, self.l_ref, s_refs, vt_refs = refs
        self.kv_ref, self.slot, self.head = kv_ref, slot, head
        self.s_ref, self.vt_ref = s_refs[at % 2], vt_refs[slot]
        self.rows = self.qt_ref.shape[1]
        self.half = self.rows // 2

    def keys(self, c):
        return self.kv_ref[self.slot, c * self.half:(c + 1) * self.half, :HEAD_SIZE]

    def chunk(self, c):
        return slice(c * self.half, (c + 1) * self.half)

    @property
    def row(self):
        return slice(self.head, self.head + 1)


class WholeStep(Step):
    def scores(self, c):
        s = dot(self.keys(c), self.qt_ref[head_rows(self.head), :])
        self.s_ref[self.chunk(c), :] = s
        return column_max(s)

    def start(self, top):
        m_old = self.m_ref[self.row, :]
        self.m = jnp.maximum(m_old, top * SCALE)
        self.correct = jnp.exp2(m_old - self.m)
        self.l = self.l_ref[self.row, :] * self.correct
        self.weights = []

    def weigh(self, c):
        p = jnp.exp2(self.s_ref[self.chunk(c), :] * SCALE - self.m)
        self.l = self.l + column_sum(p)
        self.weights.append(p.astype(jnp.bfloat16))

    def finish(self):
        o = dot(self.vt_ref[...], jnp.concatenate(self.weights, axis=0))
        at = head_rows(self.head)
        self.acc_ref[at, :] = self.acc_ref[at, :] * self.correct + o
        self.m_ref[self.row, :] = self.m
        self.l_ref[self.row, :] = self.l


class DiagonalStep(Step):
    def scores(self, c):
        half = self.half
        lower = lax.broadcasted_iota(jnp.int32, (half, half), 0) <= lax.broadcasted_iota(
            jnp.int32, (half, half), 1
        )
        qt = self.qt_ref[head_rows(self.head), :]
        if c == 0:
            near = jnp.where(lower, dot(self.keys(0), qt[:, :half]), -jnp.inf)
            over = dot(self.keys(0), qt[:, half:])
            self.s_ref[:half, :half] = near
            self.s_ref[:half, half:] = over
            return jnp.concatenate([column_max(near), column_max(over)], axis=1)
        far = jnp.where(lower, dot(self.keys(1), qt[:, half:]), -jnp.inf)
        self.s_ref[half:, half:] = far
        return jnp.concatenate([jnp.full((1, half), -jnp.inf, jnp.float32), column_max(far)], axis=1)

    def start(self, top):
        self.m = top * SCALE

    def weigh(self, c):
        half = self.half
        if c == 0:
            p = jnp.exp2(self.s_ref[:half, :] * SCALE - self.m)
            self.l0 = column_sum(p)
            self.p0 = p.astype(jnp.bfloat16)
        else:
            p = jnp.exp2(self.s_ref[half:, half:] * SCALE - self.m[:, half:])
            self.l1 = column_sum(p)
            self.p1 = p.astype(jnp.bfloat16)

    def finish(self):
        half = self.half
        at = head_rows(self.head)
        self.acc_ref[at, :half] = dot(self.vt_ref[:, :half], self.p0[:, :half])
        self.acc_ref[at, half:] = dot(
            self.vt_ref[...], jnp.concatenate([self.p0[:, half:], self.p1], axis=0)
        )
        self.m_ref[self.row, :] = self.m
        self.l_ref[self.row, :half] = self.l0[:, :half]
        self.l_ref[self.row, half:] = self.l0[:, half:] + self.l1


def run_chain(refs, kv_ref, parts):
    heads, vt_refs = refs[2].shape[0], refs[5]
    steps = []
    for kind, slot in parts:
        vt_refs[slot][...] = kv_ref[slot, :, HEAD_SIZE:].T
        steps += [kind(refs, kv_ref, slot, i, len(steps) + i) for i in range(heads)]
    top = jnp.maximum(steps[0].scores(0), steps[0].scores(1))
    for now, after in zip(steps, steps[1:] + [None]):
        now.start(top)
        tops = []
        for c in range(2):
            if after is not None:
                tops.append(after.scores(c))
            now.weigh(c)
        now.finish()
        if tops:
            top = jnp.maximum(*tops)


def local_kernel(flags, q_own, q_other, kv_ref, qt_ref, acc_ref, m_ref, l_ref, *scratch):
    b = pl.program_id(0)
    refs = (qt_ref, acc_ref, m_ref, l_ref, scratch[:2], scratch[2:])

    def turn(q_ref):
        for i in range(m_ref.shape[0]):
            qt_ref[head_rows(i), :] = q_ref[:, head_rows(i)].T

    pl.when(b == 0)(lambda: turn(q_own))
    pl.when(b == 1)(lambda: turn(q_other))
    odd = (b == 0) == (flags[0] == 1)
    pl.when(odd)(lambda: run_chain(refs, kv_ref, [(DiagonalStep, 0), (WholeStep, 1)]))
    pl.when(jnp.logical_not(odd))(lambda: run_chain(refs, kv_ref, [(DiagonalStep, 1)]))


def window_kernel(sizes, last, flags, qt_ref, *refs):
    kv_refs, refs = refs[:len(sizes)], refs[len(sizes):]
    acc_in, m_in, l_in = refs[:3]
    if last:
        own_ref, other_ref, acc_ref, m_ref, l_ref, *scratch = refs[-9:]
    else:
        acc_ref, m_ref, l_ref, *scratch = refs[3:]
    b = pl.program_id(0)
    acc_ref[...] = acc_in[...]
    m_ref[...] = m_in[...]
    l_ref[...] = l_in[...]
    work = (qt_ref, acc_ref, m_ref, l_ref, scratch[:2], scratch[2:])
    for n, (kv_ref, size) in enumerate(zip(kv_refs, sizes)):
        count = flags[1 + 2 * n + b]
        for most in range(1, size + 1):
            parts = [(WholeStep, slot) for slot in range(most)]
            pl.when(count == most)(functools.partial(run_chain, work, kv_ref, parts))
    if last:

        def write(out_ref):
            for i in range(m_ref.shape[0]):
                out = acc_ref[head_rows(i), :] / l_ref[i:i + 1, :]
                out_ref[:, head_rows(i)] = out.T.astype(out_ref.dtype)

        pl.when(b == 0)(lambda: write(own_ref))
        pl.when(b == 1)(lambda: write(other_ref))


def scratch_of(rows):
    return [
        pltpu.VMEM((rows, rows), jnp.float32),
        pltpu.VMEM((rows, rows), jnp.float32),
        pltpu.VMEM((HEAD_SIZE, rows), jnp.bfloat16),
        pltpu.VMEM((HEAD_SIZE, rows), jnp.bfloat16),
    ]


def cost(heads, rows, blocks):
    return pl.CostEstimate(
        flops=int(4 * heads * rows * rows * HEAD_SIZE * blocks),
        bytes_accessed=2 * 4 * heads * HEAD_SIZE * rows,
        transcendentals=int(heads * rows * rows * blocks),
    )


def state_specs(group, rows):
    return (
        pl.BlockSpec((group * HEAD_SIZE, rows), lambda b, flags: (b, 0)),
        pl.BlockSpec((None, group, rows), lambda b, flags: (b, 0, 0)),
    )


def pair_spec(pair):
    return pl.BlockSpec(pair.shape, lambda b, flags: (0, 0, 0))


def local_attention(flags, queries, received, pair, group, kv_heads, h):
    rows = queries.shape[0]
    span = group * HEAD_SIZE
    wide, thin = state_specs(group, rows)
    grid_spec = pltpu.PrefetchScalarGridSpec(
        num_scalar_prefetch=1,
        grid=(2,),
        in_specs=[
            pl.BlockSpec((rows, span), lambda b, flags: (0, flags[0] * kv_heads + h)),
            pl.BlockSpec((rows, span), lambda b, flags: (0, h)),
            pair_spec(pair),
        ],
        out_specs=[wide, wide, thin, thin],
        scratch_shapes=scratch_of(rows),
    )
    stats = jax.ShapeDtypeStruct((2, group, rows), jnp.float32)
    return pl.pallas_call(
        local_kernel,
        grid_spec=grid_spec,
        out_shape=[
            jax.ShapeDtypeStruct((2 * span, rows), jnp.bfloat16),
            jax.ShapeDtypeStruct((2 * span, rows), jnp.float32),
            stats,
            stats,
        ],
        compiler_params=pltpu.CompilerParams(vmem_limit_bytes=VMEM_LIMIT),
        cost_estimate=cost(2 * group, rows, 1),
        name=f"attend_local_{h}",
    )(flags, queries, received, pair)


def window_attention(flags, qt, pairs, state, group, name):
    rows = qt.shape[1]
    wide, thin = state_specs(group, rows)
    grid_spec = pltpu.PrefetchScalarGridSpec(
        num_scalar_prefetch=1,
        grid=(2,),
        in_specs=[wide, *[pair_spec(pair) for pair in pairs], wide, thin, thin],
        out_specs=[wide, thin, thin],
        scratch_shapes=scratch_of(rows),
    )
    sizes = [pair.shape[0] for pair in pairs]
    return pl.pallas_call(
        functools.partial(window_kernel, sizes, False),
        grid_spec=grid_spec,
        out_shape=[jax.ShapeDtypeStruct(a.shape, a.dtype) for a in state],
        compiler_params=pltpu.CompilerParams(vmem_limit_bytes=VMEM_LIMIT),
        cost_estimate=cost(2 * group, rows, sum(sizes)),
        name=name,
    )(flags, qt, *pairs, *state)


def last_attention(flags, qt, pairs, state, out, width, group, kv_heads, h, name):
    rows = qt.shape[1]
    span = group * HEAD_SIZE
    wide, thin = state_specs(group, rows)
    grid_spec = pltpu.PrefetchScalarGridSpec(
        num_scalar_prefetch=1,
        grid=(2,),
        in_specs=[
            wide, *[pair_spec(pair) for pair in pairs], wide, thin, thin,
            *[pl.BlockSpec(memory_space=pl.ANY) for _ in out],
        ],
        out_specs=[
            pl.BlockSpec((rows, span), lambda b, flags: (0, flags[0] * kv_heads + h)),
            pl.BlockSpec((rows, span), lambda b, flags: (0, 0)),
        ],
        scratch_shapes=[
            pltpu.VMEM((span, rows), jnp.float32),
            pltpu.VMEM((group, rows), jnp.float32),
            pltpu.VMEM((group, rows), jnp.float32),
            *scratch_of(rows),
        ],
    )
    sizes = [pair.shape[0] for pair in pairs]
    return pl.pallas_call(
        functools.partial(window_kernel, sizes, True),
        grid_spec=grid_spec,
        out_shape=[
            jax.ShapeDtypeStruct((rows, width), jnp.bfloat16),
            jax.ShapeDtypeStruct((rows, span), jnp.bfloat16),
        ],
        input_output_aliases={5 + len(pairs): 0} if out else {},
        compiler_params=pltpu.CompilerParams(vmem_limit_bytes=VMEM_LIMIT),
        cost_estimate=cost(2 * group, rows, sum(sizes)),
        name=name,
    )(flags, qt, *pairs, *state, *out)


def on_device(queries, keys, values, prefix_spans):
    rows, width = queries.shape
    length = lax.axis_size("ctx")
    kv_local = keys.shape[1] // HEAD_SIZE
    shared = kv_local % 2 == 1
    kv_heads, group = (kv_local, GROUP // 2) if shared else (kv_local // 2, GROUP)
    q_width, kv_width = width // 2, kv_heads * HEAD_SIZE

    position = lax.axis_index("ctx")
    core = position % 2
    lower = (position // 2) % 2 == 0
    swap = [(i, i ^ 1) for i in range(length)]
    across = [(i, i ^ 2) for i in range(length)]
    ahead = [(i, i + 4) for i in range(length - 4)]

    def halves(a):
        if shared:
            return a, a
        low, high = a[:, :kv_width], a[:, kv_width:]
        return jnp.where(core == 0, low, high), jnp.where(core == 0, high, low)

    k_mine, k_theirs = halves(keys)
    v_mine, v_theirs = halves(values)
    span_columns = jnp.broadcast_to(prefix_spans.astype(jnp.bfloat16), (rows, HEAD_SIZE))
    kv_got = moved(jnp.concatenate([k_theirs, v_theirs, span_columns], axis=1), swap)
    q_got = moved(lax.dynamic_slice_in_dim(queries, (1 - core) * q_width, q_width, 1), swap)

    def pair_of(h):
        at = head_rows(h)
        mine = jnp.concatenate([k_mine[:, at], v_mine[:, at]], axis=1)
        got = jnp.concatenate([kv_got[:, at], kv_got[:, kv_width:][:, at]], axis=1)
        return jnp.stack([jnp.where(core == 1, mine, got), jnp.where(core == 1, got, mine)])

    pairs = [pair_of(h) for h in range(kv_heads)]

    reach_own = jnp.minimum(prefix_spans[0], position)
    reach_other = jnp.minimum(kv_got[0, 2 * kv_width].astype(jnp.int32), position ^ 1)

    def counts(distance):
        first = 2 * distance - 1
        return [
            jnp.clip(reach_own - first - core + 1, 0, 2),
            jnp.clip(reach_other - first - (1 - core) + 1, 0, 2),
        ]

    local_flags = core[None].astype(jnp.int32)
    near_flags = jnp.stack([core, *counts(1), *counts(2)]).astype(jnp.int32)
    far_flags = jnp.stack([core, *counts(3), *counts(4)]).astype(jnp.int32)

    def across_of(pair, second):
        return moved(jnp.where(lower, pair, second), across)

    heads = range(kv_heads)
    state, first, second, third = {}, {}, {}, {}
    second[0] = moved(pairs[0], ahead)
    state[0] = local_attention(local_flags, queries, q_got, pairs[0], group, kv_heads, 0)
    for h in heads[1:]:
        (second[h - 1], state[h - 1]) = lax.optimization_barrier((second[h - 1], state[h - 1]))
        second[h] = moved(pairs[h], ahead)
        first[h - 1] = across_of(pairs[h - 1], second[h - 1])
        state[h] = local_attention(local_flags, queries, q_got, pairs[h], group, kv_heads, h)
    h = kv_heads - 1
    (second[h], first, state[h]) = lax.optimization_barrier((second[h], first, state[h]))
    first[h] = across_of(pairs[h], second[h])

    fourth = None
    for h in heads:
        third[h] = moved(first[h], ahead)
        if h == kv_heads - 1:
            fourth = moved(jnp.stack([second[g][0] for g in heads]), ahead)
        qt, *old = state[h]
        new = window_attention(near_flags, qt, [first[h], second[h]], old, group, f"attend_near_{h}")
        state[h] = [qt, *new]
        if h + 1 < kv_heads:
            (first[h + 1], state[h]) = lax.optimization_barrier((first[h + 1], state[h]))

    out = None
    returned = []
    for h in heads:
        qt, *old = state[h]
        out, other = last_attention(
            far_flags, qt, [third[h], fourth[h:h + 1]], old, [out] if h else [], width,
            group, kv_heads, h, f"attend_far_{h}",
        )
        returned.append(moved(other, swap))
    for h in heads:
        at = (1 - core) * q_width + h * group * HEAD_SIZE
        out = lax.dynamic_update_slice_in_dim(out, returned[h], at, 1)
    return out


def solution(mesh):
    placed = (P("ctx", "tp"), P("ctx", "tp"), P("ctx", "tp"), P("ctx"))
    return jax.shard_map(
        on_device, mesh=mesh, in_specs=placed, out_specs=P("ctx", "tp"), check_vma=False
    )
```

```python
import functools
import math

import jax
import jax.numpy as jnp
from jax import lax
from jax.experimental import pallas as pl
from jax.experimental.pallas import tpu as pltpu
from jax.sharding import PartitionSpec as P

QUERY_HEAD_COUNT = 64
KEY_VALUE_HEADS = 8
HEAD_SIZE = 128
GROUP = QUERY_HEAD_COUNT // KEY_VALUE_HEADS
SCALE = math.log2(math.e) / math.sqrt(HEAD_SIZE)
MIB = 1024 * 1024
VMEM_LIMIT = 16 * MIB
QUERY_VMEM_LIMIT = 40 * MIB
CUT_VMEM_LIMIT = 60 * MIB


def moved(shard, pairs):
    return lax.ppermute(shard, "ctx", pairs)


def head_rows(i):
    return slice(i * HEAD_SIZE, (i + 1) * HEAD_SIZE)


def column_max(s):
    return jnp.max(s, axis=0, keepdims=True)


def column_sum(s):
    return jnp.sum(s, axis=0, keepdims=True)


def dot(a, b):
    return jnp.dot(a, b, preferred_element_type=jnp.float32)


class Step:
    def __init__(self, refs, kv_ref, slot, head, at):
        self.qt_ref, self.acc_ref, self.m_ref, self.l_ref, s_refs, vt_refs = refs
        self.kv_ref, self.slot, self.head = kv_ref, slot, head
        self.s_ref, self.vt_ref = s_refs[at % 2], vt_refs[slot]
        self.rows = self.qt_ref.shape[1]
        self.half = self.rows // 2

    def keys(self, c):
        return self.kv_ref[self.slot, c * self.half:(c + 1) * self.half, :HEAD_SIZE]

    def chunk(self, c):
        return slice(c * self.half, (c + 1) * self.half)

    @property
    def row(self):
        return slice(self.head, self.head + 1)


class WholeStep(Step):
    def scores(self, c):
        s = dot(self.keys(c), self.qt_ref[head_rows(self.head), :])
        self.s_ref[self.chunk(c), :] = s
        return column_max(s)

    def start(self, top):
        m_old = self.m_ref[self.row, :]
        self.m = jnp.maximum(m_old, top * SCALE)
        self.correct = jnp.exp2(m_old - self.m)
        self.l = self.l_ref[self.row, :] * self.correct
        self.weights = []

    def weigh(self, c):
        p = jnp.exp2(self.s_ref[self.chunk(c), :] * SCALE - self.m)
        self.l = self.l + column_sum(p)
        self.weights.append(p.astype(jnp.bfloat16))

    def finish(self):
        o = dot(self.vt_ref[...], jnp.concatenate(self.weights, axis=0))
        at = head_rows(self.head)
        self.acc_ref[at, :] = self.acc_ref[at, :] * self.correct + o
        self.m_ref[self.row, :] = self.m
        self.l_ref[self.row, :] = self.l


class DiagonalStep(Step):
    def scores(self, c):
        half = self.half
        lower = lax.broadcasted_iota(jnp.int32, (half, half), 0) <= lax.broadcasted_iota(
            jnp.int32, (half, half), 1
        )
        qt = self.qt_ref[head_rows(self.head), :]
        if c == 0:
            near = jnp.where(lower, dot(self.keys(0), qt[:, :half]), -jnp.inf)
            over = dot(self.keys(0), qt[:, half:])
            self.s_ref[:half, :half] = near
            self.s_ref[:half, half:] = over
            return jnp.concatenate([column_max(near), column_max(over)], axis=1)
        far = jnp.where(lower, dot(self.keys(1), qt[:, half:]), -jnp.inf)
        self.s_ref[half:, half:] = far
        return jnp.concatenate([jnp.full((1, half), -jnp.inf, jnp.float32), column_max(far)], axis=1)

    def start(self, top):
        self.m = top * SCALE

    def weigh(self, c):
        half = self.half
        if c == 0:
            p = jnp.exp2(self.s_ref[:half, :] * SCALE - self.m)
            self.l0 = column_sum(p)
            self.p0 = p.astype(jnp.bfloat16)
        else:
            p = jnp.exp2(self.s_ref[half:, half:] * SCALE - self.m[:, half:])
            self.l1 = column_sum(p)
            self.p1 = p.astype(jnp.bfloat16)

    def finish(self):
        half = self.half
        at = head_rows(self.head)
        self.acc_ref[at, :half] = dot(self.vt_ref[:, :half], self.p0[:, :half])
        self.acc_ref[at, half:] = dot(
            self.vt_ref[...], jnp.concatenate([self.p0[:, half:], self.p1], axis=0)
        )
        self.m_ref[self.row, :] = self.m
        self.l_ref[self.row, :half] = self.l0[:, :half]
        self.l_ref[self.row, half:] = self.l0[:, half:] + self.l1


def run_chain(refs, kv_ref, parts):
    heads, vt_refs = refs[2].shape[0], refs[5]
    steps = []
    for kind, slot in parts:
        vt_refs[slot][...] = kv_ref[slot, :, HEAD_SIZE:].T
        steps += [kind(refs, kv_ref, slot, i, len(steps) + i) for i in range(heads)]
    top = jnp.maximum(steps[0].scores(0), steps[0].scores(1))
    for now, after in zip(steps, steps[1:] + [None]):
        now.start(top)
        tops = []
        for c in range(2):
            if after is not None:
                tops.append(after.scores(c))
            now.weigh(c)
        now.finish()
        if tops:
            top = jnp.maximum(*tops)


def chains_for(work, b):
    qt_ref, acc_ref, m_ref, l_ref, *rest = work
    return (qt_ref.at[b], acc_ref.at[b], m_ref.at[b], l_ref.at[b], rest[:2], rest[2:])


def local_kernel(
    kv_heads, h, flags, queries, received, kv_ref, qt_ref, acc_ref, m_ref, l_ref, q_buf, arrived, *scratch
):
    core = flags[0]
    span = q_buf.shape[2]
    work = (qt_ref, acc_ref, m_ref, l_ref, *scratch)
    own_at = pl.multiple_of((core * kv_heads + h) * span, span)
    sources = [queries.at[:, pl.ds(own_at, span)], received.at[:, h * span:(h + 1) * span]]
    copies = [pltpu.make_async_copy(sources[i], q_buf.at[i], arrived.at[i]) for i in range(2)]
    for copy in copies:
        copy.start()
    copies[0].wait()
    copies[1].wait()

    def block(b, carry):
        refs = chains_for(work, b)
        for i in range(span // HEAD_SIZE):
            refs[0][head_rows(i), :] = q_buf[b, :, head_rows(i)].T
        odd = (b == 0) == (core == 1)
        pl.when(odd)(lambda: run_chain(refs, kv_ref, [(DiagonalStep, 0), (WholeStep, 1)]))
        pl.when(jnp.logical_not(odd))(lambda: run_chain(refs, kv_ref, [(DiagonalStep, 1)]))
        return carry

    lax.fori_loop(0, 2, block, 0)


def add_pairs(flags, work, kv_refs, b):
    refs = chains_for(work, b)
    for n, kv_ref in enumerate(kv_refs):
        count = flags[1 + 2 * n + b]
        for most in range(1, kv_ref.shape[0] + 1):
            parts = [(WholeStep, slot) for slot in range(most)]
            pl.when(count == most)(functools.partial(run_chain, refs, kv_ref, parts))
    return refs


def window_kernel(pieces, flags, qt_ref, *refs):
    kv_refs, refs = refs[:pieces], refs[pieces + 3:]
    work = (qt_ref, *refs)

    def block(b, carry):
        add_pairs(flags, work, kv_refs, b)
        return carry

    lax.fori_loop(0, 2, block, 0)


def last_kernel(pieces, kv_heads, h, flags, qt_ref, *refs):
    kv_refs, state, refs = refs[:pieces], refs[pieces:pieces + 3], refs[pieces + 3:]
    if h:
        _, before, out, other, stage, sent, *scratch = refs
    else:
        out, other, stage, sent, *scratch = refs
    core = flags[0]
    span = stage.shape[2]
    own_at = pl.multiple_of((core * kv_heads + h) * span, span)
    copies = [
        pltpu.make_async_copy(stage.at[0], out.at[:, pl.ds(own_at, span)], sent.at[0]),
        pltpu.make_async_copy(stage.at[1], other, sent.at[1]),
    ]
    if h:
        before_at = pl.multiple_of(((1 - core) * kv_heads + h - 1) * span, span)
        copies.append(pltpu.make_async_copy(before, out.at[:, pl.ds(before_at, span)], sent.at[2]))
        copies[2].start()
    work = (qt_ref, *state, *scratch)

    def block(b, carry):
        _, acc_ref, _, l_ref, *_ = add_pairs(flags, work, kv_refs, b)
        for i in range(span // HEAD_SIZE):
            result = acc_ref[head_rows(i), :] / l_ref[i:i + 1, :]
            stage[b, :, head_rows(i)] = result.T.astype(stage.dtype)
        return carry

    lax.fori_loop(0, 2, block, 0)
    copies[0].start()
    copies[1].start()
    for copy in copies:
        copy.wait()


def cut_kernel(flags, queries, out, done):
    width = out.shape[1]
    at = pl.multiple_of((1 - flags[0]) * width, width)
    copy = pltpu.make_async_copy(queries.at[:, pl.ds(at, width)], out, done.at[0])
    copy.start()
    copy.wait()


def place_kernel(at_block, blocks, flags, piece, _, out, done):
    width = piece.shape[1]
    at = pl.multiple_of(((1 - flags[0]) * blocks + at_block) * width, width)
    copy = pltpu.make_async_copy(piece, out.at[:, pl.ds(at, width)], done.at[0])
    copy.start()
    copy.wait()


SMEM = pl.BlockSpec(memory_space=pltpu.SMEM)
VMEM = pl.BlockSpec(memory_space=pltpu.VMEM)
HBM = pl.BlockSpec(memory_space=pltpu.HBM)


def scratch_of(rows):
    return [
        pltpu.VMEM((rows, rows), jnp.float32),
        pltpu.VMEM((rows, rows), jnp.float32),
        pltpu.VMEM((HEAD_SIZE, rows), jnp.bfloat16),
        pltpu.VMEM((HEAD_SIZE, rows), jnp.bfloat16),
    ]


def params_of(heads, rows, blocks, limit=VMEM_LIMIT):
    return dict(
        compiler_params=pltpu.CompilerParams(vmem_limit_bytes=limit),
        cost_estimate=pl.CostEstimate(
            flops=int(4 * heads * rows * rows * HEAD_SIZE * blocks),
            bytes_accessed=4 * heads * HEAD_SIZE * rows,
            transcendentals=int(heads * rows * rows * blocks),
        ),
    )


def local_attention(flags, queries, received, pair, group, kv_heads, h):
    rows = queries.shape[0]
    span = group * HEAD_SIZE
    stats = jax.ShapeDtypeStruct((2, group, rows), jnp.float32)
    return pl.pallas_call(
        functools.partial(local_kernel, kv_heads, h),
        in_specs=[SMEM, HBM, HBM, VMEM],
        out_specs=[VMEM] * 4,
        out_shape=[
            jax.ShapeDtypeStruct((2, span, rows), jnp.bfloat16),
            jax.ShapeDtypeStruct((2, span, rows), jnp.float32),
            stats,
            stats,
        ],
        scratch_shapes=[
            pltpu.VMEM((2, rows, span), jnp.bfloat16),
            pltpu.SemaphoreType.DMA((2,)),
            *scratch_of(rows),
        ],
        name=f"attend_local_{h}",
        **params_of(2 * group, rows, 1, QUERY_VMEM_LIMIT),
    )(flags, queries, received, pair)


def window_attention(flags, qt, pairs, state, group, name):
    rows = qt.shape[2]
    return pl.pallas_call(
        functools.partial(window_kernel, len(pairs)),
        in_specs=[SMEM] + [VMEM] * (4 + len(pairs)),
        out_specs=[VMEM] * 3,
        out_shape=[jax.ShapeDtypeStruct(a.shape, a.dtype) for a in state],
        scratch_shapes=scratch_of(rows),
        input_output_aliases={2 + len(pairs) + i: i for i in range(3)},
        name=name,
        **params_of(2 * group, rows, 2 * len(pairs)),
    )(flags, qt, *pairs, *state)


def last_attention(flags, qt, pairs, state, placed, width, group, kv_heads, h, name):
    rows = qt.shape[2]
    span = group * HEAD_SIZE
    return pl.pallas_call(
        functools.partial(last_kernel, len(pairs), kv_heads, h),
        in_specs=[SMEM] + [VMEM] * (4 + len(pairs)) + [HBM] * len(placed),
        out_specs=[HBM, HBM],
        out_shape=[
            jax.ShapeDtypeStruct((rows, width), jnp.bfloat16),
            jax.ShapeDtypeStruct((rows, span), jnp.bfloat16),
        ],
        scratch_shapes=[
            pltpu.VMEM((2, rows, span), jnp.bfloat16),
            pltpu.SemaphoreType.DMA((3,)),
            *scratch_of(rows),
        ],
        input_output_aliases={5 + len(pairs): 0} if placed else {},
        name=name,
        **params_of(2 * group, rows, 2 * len(pairs)),
    )(flags, qt, *pairs, *state, *placed)


def cut_out(flags, queries, width):
    return pl.pallas_call(
        cut_kernel,
        in_specs=[SMEM, HBM],
        out_specs=HBM,
        out_shape=jax.ShapeDtypeStruct((queries.shape[0], width), queries.dtype),
        scratch_shapes=[pltpu.SemaphoreType.DMA((1,))],
        compiler_params=pltpu.CompilerParams(vmem_limit_bytes=CUT_VMEM_LIMIT),
        name="cut_queries",
    )(flags, queries)


def put_in(flags, piece, out, at_block, blocks):
    return pl.pallas_call(
        functools.partial(place_kernel, at_block, blocks),
        in_specs=[SMEM, HBM, HBM],
        out_specs=HBM,
        out_shape=jax.ShapeDtypeStruct(out.shape, out.dtype),
        scratch_shapes=[pltpu.SemaphoreType.DMA((1,))],
        input_output_aliases={2: 0},
        name="place_result",
    )(flags, piece, out)


def on_device(queries, keys, values, prefix_spans):
    rows, width = queries.shape
    length = lax.axis_size("ctx")
    kv_local = keys.shape[1] // HEAD_SIZE
    shared = kv_local % 2 == 1
    kv_heads, group = (kv_local, GROUP // 2) if shared else (kv_local // 2, GROUP)
    q_width, kv_width = width // 2, kv_heads * HEAD_SIZE

    position = lax.axis_index("ctx")
    core = position % 2
    lower = (position // 2) % 2 == 0
    swap = [(i, i ^ 1) for i in range(length)]
    across = [(i, i ^ 2) for i in range(length)]
    ahead = [(i, i + 4) for i in range(length - 4)]

    def halves(a):
        if shared:
            return a, a
        low, high = a[:, :kv_width], a[:, kv_width:]
        return jnp.where(core == 0, low, high), jnp.where(core == 0, high, low)

    k_mine, k_theirs = halves(keys)
    v_mine, v_theirs = halves(values)
    span_columns = jnp.broadcast_to(prefix_spans.astype(jnp.bfloat16), (rows, HEAD_SIZE))
    kv_sent = jnp.concatenate([k_theirs, v_theirs, span_columns], axis=1)
    core_flag = core[None].astype(jnp.int32)
    kv_got, q_flag = lax.optimization_barrier((moved(kv_sent, swap), core_flag))
    q_got = moved(cut_out(q_flag, queries, q_width), swap)

    def pair_of(h):
        at = head_rows(h)
        mine = jnp.concatenate([k_mine[:, at], v_mine[:, at]], axis=1)
        got = jnp.concatenate([kv_got[:, at], kv_got[:, kv_width:][:, at]], axis=1)
        return jnp.stack([jnp.where(core == 1, mine, got), jnp.where(core == 1, got, mine)])

    pairs = [pair_of(h) for h in range(kv_heads)]

    reach_own = jnp.minimum(prefix_spans[0], position)
    reach_other = jnp.minimum(kv_got[0, 2 * kv_width].astype(jnp.int32), position ^ 1)

    def counts(distance):
        first = 2 * distance - 1
        return [
            jnp.clip(reach_own - first - core + 1, 0, 2),
            jnp.clip(reach_other - first - (1 - core) + 1, 0, 2),
        ]

    local_flags = core_flag
    near_flags = jnp.stack([core, *counts(1), *counts(2)]).astype(jnp.int32)
    far_flags = jnp.stack([core, *counts(3), *counts(4)]).astype(jnp.int32)

    def across_of(pair, second):
        return moved(jnp.where(lower, pair, second), across)

    heads = range(kv_heads)
    state, first, second, third = {}, {}, {}, {}
    second[0] = moved(pairs[0], ahead)
    state[0] = local_attention(local_flags, queries, q_got, pairs[0], group, kv_heads, 0)
    for h in heads[1:]:
        (second[h - 1], state[h - 1]) = lax.optimization_barrier((second[h - 1], state[h - 1]))
        second[h] = moved(pairs[h], ahead)
        first[h - 1] = across_of(pairs[h - 1], second[h - 1])
        state[h] = local_attention(local_flags, queries, q_got, pairs[h], group, kv_heads, h)
    h = kv_heads - 1
    (second[h], first, state[h]) = lax.optimization_barrier((second[h], first, state[h]))
    first[h] = across_of(pairs[h], second[h])

    fourth = None
    for h in heads:
        third[h] = moved(first[h], ahead)
        if h == kv_heads - 1:
            fourth = moved(jnp.stack([second[g][0] for g in heads]), ahead)
        qt, *old = state[h]
        new = window_attention(near_flags, qt, [first[h], second[h]], old, group, f"attend_near_{h}")
        state[h] = [qt, *new]
        if h + 1 < kv_heads:
            (first[h + 1], state[h]) = lax.optimization_barrier((first[h + 1], state[h]))

    out = None
    for h in heads:
        qt, *old = state[h]
        placed = [out, returned] if h else []
        out, other = last_attention(
            far_flags, qt, [third[h], fourth[h:h + 1]], old, placed, width,
            group, kv_heads, h, f"attend_far_{h}",
        )
        returned = moved(other, swap)
    return put_in(core_flag, returned, out, kv_heads - 1, kv_heads)


def solution(mesh):
    placed = (P("ctx", "tp"), P("ctx", "tp"), P("ctx", "tp"), P("ctx"))
    return jax.shard_map(
        on_device, mesh=mesh, in_specs=placed, out_specs=P("ctx", "tp"), check_vma=False
    )
```

```python
import functools
import math

import jax
import jax.numpy as jnp
from jax import lax
from jax.experimental import pallas as pl
from jax.experimental.pallas import tpu as pltpu
from jax.sharding import PartitionSpec as P

QUERY_HEAD_COUNT = 64
KEY_VALUE_HEADS = 8
HEAD_SIZE = 128
GROUP = QUERY_HEAD_COUNT // KEY_VALUE_HEADS
SCALE = math.log2(math.e) / math.sqrt(HEAD_SIZE)
EXPONENT_ROOM = 100.0
ONES_ROWS = 16
MIB = 1024 * 1024
VMEM_LIMIT = 16 * MIB
CUT_VMEM_LIMIT = 57 * MIB


def moved(shard, pairs):
    return lax.ppermute(shard, "ctx", pairs)


def head_rows(i):
    return slice(i * HEAD_SIZE, (i + 1) * HEAD_SIZE)


def column_max(s):
    return jnp.max(s, axis=0, keepdims=True)


def column_sum(s):
    return jnp.sum(s, axis=0, keepdims=True)


def dot(a, b):
    return jnp.dot(a, b, preferred_element_type=jnp.float32)


class Step:
    def __init__(self, refs, kv_ref, slot, head, at):
        self.qt_ref, self.acc_ref, self.m_ref, self.l_ref, s_refs, vt_refs = refs
        self.kv_ref, self.slot, self.head = kv_ref, slot, head
        self.s_ref, self.vt_ref = s_refs[at % 2], vt_refs[slot]
        self.rows = self.qt_ref.shape[1]
        self.half = self.rows // 2

    def keys(self, c):
        return self.kv_ref[self.slot, c * self.half:(c + 1) * self.half, :HEAD_SIZE]

    def chunk(self, c):
        return slice(c * self.half, (c + 1) * self.half)

    @property
    def row(self):
        return slice(self.head, self.head + 1)


class DiagonalStep(Step):
    def scores(self, c):
        half = self.half
        lower = lax.broadcasted_iota(jnp.int32, (half, half), 0) <= lax.broadcasted_iota(
            jnp.int32, (half, half), 1
        )
        qt = self.qt_ref[head_rows(self.head), :]
        if c == 0:
            near = jnp.where(lower, dot(self.keys(0), qt[:, :half]), -jnp.inf)
            over = dot(self.keys(0), qt[:, half:])
            self.s_ref[:half, :half] = near
            self.s_ref[:half, half:] = over
            return jnp.concatenate([column_max(near), column_max(over)], axis=1)
        far = jnp.where(lower, dot(self.keys(1), qt[:, half:]), -jnp.inf)
        self.s_ref[half:, half:] = far
        return jnp.concatenate([jnp.full((1, half), -jnp.inf, jnp.float32), column_max(far)], axis=1)

    def start(self, top):
        self.m = top * SCALE

    def weigh(self, c):
        half = self.half
        if c == 0:
            p = jnp.exp2(self.s_ref[:half, :] * SCALE - self.m)
            self.l0 = column_sum(p)
            self.p0 = p.astype(jnp.bfloat16)
        else:
            p = jnp.exp2(self.s_ref[half:, half:] * SCALE - self.m[:, half:])
            self.l1 = column_sum(p)
            self.p1 = p.astype(jnp.bfloat16)

    def finish(self):
        half = self.half
        at = head_rows(self.head)
        self.acc_ref[at, :half] = dot(self.vt_ref[:HEAD_SIZE, :half], self.p0[:, :half])
        self.acc_ref[at, half:] = dot(
            self.vt_ref[:HEAD_SIZE, :], jnp.concatenate([self.p0[:, half:], self.p1], axis=0)
        )
        self.m_ref[self.row, :] = self.m
        self.l_ref[self.row, :half] = self.l0[:, :half]
        self.l_ref[self.row, half:] = self.l0[:, half:] + self.l1


def run_diagonal(refs, kv_ref, slot):
    refs[5][slot][:HEAD_SIZE, :] = kv_ref[slot, :, HEAD_SIZE:].T
    steps = [DiagonalStep(refs, kv_ref, slot, i, i) for i in range(refs[2].shape[0])]
    top = jnp.maximum(steps[0].scores(0), steps[0].scores(1))
    for now, after in zip(steps, steps[1:] + [None]):
        now.start(top)
        tops = []
        for c in range(2):
            if after is not None:
                tops.append(after.scores(c))
            now.weigh(c)
        now.finish()
        if tops:
            top = jnp.maximum(*tops)


def run_bounded(refs, kv_ref, slots):
    qt_ref, acc_ref, m_ref, l_ref, _, vt_refs = refs
    heads, rows = m_ref.shape
    half = rows // 2

    def weights(slot, i):
        qt = qt_ref[head_rows(i), :]
        m = m_ref[i:i + 1, :]
        parts = []
        for c in range(2):
            s = dot(kv_ref[slot, c * half:(c + 1) * half, :HEAD_SIZE], qt)
            parts.append(jnp.exp2(s * SCALE - m).astype(jnp.bfloat16))
        return jnp.concatenate(parts, axis=0)

    def add(slot, i, w):
        o = dot(vt_refs[slot][...], w)
        acc_ref[head_rows(i), :] += o[:HEAD_SIZE, :]
        l_ref[i:i + 1, :] += o[HEAD_SIZE:HEAD_SIZE + 1, :]

    waiting = None
    for slot in slots:
        vt_refs[slot][:HEAD_SIZE, :] = kv_ref[slot, :, HEAD_SIZE:].T
        for i in range(heads):
            w = weights(slot, i)
            if waiting is not None:
                add(*waiting)
            waiting = (slot, i, w)
    add(*waiting)


def run_exact(refs, kv_ref, slots):
    qt_ref, acc_ref, m_ref, l_ref, _, vt_refs = refs
    for slot in slots:
        vt_refs[slot][:HEAD_SIZE, :] = kv_ref[slot, :, HEAD_SIZE:].T

        def head(i, carry, slot=slot):
            at = pl.ds(pl.multiple_of(i * HEAD_SIZE, HEAD_SIZE), HEAD_SIZE)
            row = pl.ds(i, 1)
            s = dot(kv_ref[slot, :, :HEAD_SIZE], qt_ref[at, :]) * SCALE
            m_old = m_ref[row, :]
            m = jnp.maximum(m_old, column_max(s))
            correct = jnp.exp2(m_old - m)
            o = dot(vt_refs[slot][...], jnp.exp2(s - m).astype(jnp.bfloat16))
            acc_ref[at, :] = acc_ref[at, :] * correct + o[:HEAD_SIZE, :]
            l_ref[row, :] = l_ref[row, :] * correct + o[HEAD_SIZE:HEAD_SIZE + 1, :]
            m_ref[row, :] = m
            return carry

        lax.fori_loop(0, m_ref.shape[0], head, 0)


def run_whole(refs, bound_ref, kv_ref, slots):
    longest = 0.0
    for slot in slots:
        k = kv_ref[slot, :, :HEAD_SIZE].astype(jnp.float32)
        longest = jnp.maximum(longest, jnp.max(jnp.sum(k * k, axis=1, keepdims=True)))
    longest = jnp.sqrt(jnp.full((1, 1), longest, jnp.float32))
    bounded = jnp.max(bound_ref[...] * longest - refs[2][...]) <= EXPONENT_ROOM
    pl.when(bounded)(lambda: run_bounded(refs, kv_ref, slots))
    pl.when(jnp.logical_not(bounded))(lambda: run_exact(refs, kv_ref, slots))


def fill_ones(vt_refs):
    for vt_ref in vt_refs:
        vt_ref[HEAD_SIZE:, :] = jnp.ones((ONES_ROWS, vt_ref.shape[1]), jnp.bfloat16)


def refs_for(work, b):
    qt_ref, acc_ref, m_ref, l_ref, *rest = work
    return (qt_ref.at[b], acc_ref.at[b], m_ref.at[b], l_ref.at[b], rest[:2], rest[2:])


def local_kernel(
    flags, own, received, kv_ref, qt_ref, bound_ref, acc_ref, m_ref, l_ref, *scratch
):
    core = flags[0]
    work = (qt_ref, acc_ref, m_ref, l_ref, *scratch)
    fill_ones(scratch[2:])

    def turn(b, q_ref):
        for i in range(q_ref.shape[1] // HEAD_SIZE):
            qt = q_ref[:, head_rows(i)].T
            qt_ref[b, head_rows(i), :] = qt
            wide = qt.astype(jnp.float32)
            bound_ref[b, i:i + 1, :] = jnp.sqrt(column_sum(wide * wide)) * (SCALE * 1.01)

    turn(0, own)
    turn(1, received)

    def block(b, carry):
        refs = refs_for(work, b)
        odd = (b == 0) == (core == 1)
        pl.when(odd)(lambda: run_diagonal(refs, kv_ref, 0))
        pl.when(jnp.logical_not(odd))(lambda: run_diagonal(refs, kv_ref, 1))
        pl.when(odd)(lambda: run_whole(refs, bound_ref.at[b], kv_ref, [1]))
        return carry

    lax.fori_loop(0, 2, block, 0)


def add_pairs(flags, work, bound_ref, kv_refs, sizes, b):
    refs = refs_for(work, b)
    for n, kv_ref in enumerate(kv_refs):
        count = flags[1 + 2 * n + b]
        for most in range(1, sizes[n] + 1):
            slots = list(range(most))
            pl.when(count == most)(functools.partial(run_whole, refs, bound_ref.at[b], kv_ref, slots))
    return refs


def window_kernel(pieces, flags, qt_ref, bound_ref, *refs):
    kv_refs, refs = refs[:pieces], refs[pieces + 3:]
    work = (qt_ref, *refs)
    fill_ones(refs[5:])

    def block(b, carry):
        add_pairs(flags, work, bound_ref, kv_refs, (2, 2), b)
        return carry

    lax.fori_loop(0, 2, block, 0)


def last_kernel(pieces, kv_heads, h, flags, qt_ref, bound_ref, *refs):
    kv_refs, state, refs = refs[:pieces], refs[pieces:pieces + 3], refs[pieces + 3:]
    out, other, stage, sent, *scratch = refs[1:] if h else refs
    core = flags[0]
    span = stage.shape[2]
    own_at = pl.multiple_of((core * kv_heads + h) * span, span)
    copies = [
        pltpu.make_async_copy(stage.at[0], out.at[:, pl.ds(own_at, span)], sent.at[0]),
        pltpu.make_async_copy(stage.at[1], other, sent.at[1]),
    ]
    work = (qt_ref, *state, *scratch)
    fill_ones(scratch[2:])

    def block(b, carry):
        _, acc_ref, _, l_ref, *_ = add_pairs(flags, work, bound_ref, kv_refs, (2, 1), b)
        for i in range(span // HEAD_SIZE):
            result = acc_ref[head_rows(i), :] / l_ref[i:i + 1, :]
            stage[b, :, head_rows(i)] = result.T.astype(stage.dtype)
        return carry

    lax.fori_loop(0, 2, block, 0)
    copies[0].start()
    copies[1].start()
    for copy in copies:
        copy.wait()


def cut_kernel(flags, queries, own, other, done):
    width = own.shape[1]
    copies = []
    for i, (side, part) in enumerate([(1 - flags[0], other), (flags[0], own)]):
        at = pl.multiple_of(side * width, width)
        copies.append(pltpu.make_async_copy(queries.at[:, pl.ds(at, width)], part, done.at[i]))
    for copy in copies:
        copy.start()
    for copy in copies:
        copy.wait()


def place_kernel(flags, *refs):
    *pieces, _, out, done = refs
    width = pieces[0].shape[1]
    copies = []
    for i, piece in enumerate(pieces):
        at = pl.multiple_of(((1 - flags[0]) * len(pieces) + i) * width, width)
        copies.append(pltpu.make_async_copy(piece, out.at[:, pl.ds(at, width)], done.at[i]))
    for copy in copies:
        copy.start()
    for copy in copies:
        copy.wait()


SMEM = pl.BlockSpec(memory_space=pltpu.SMEM)
VMEM = pl.BlockSpec(memory_space=pltpu.VMEM)
HBM = pl.BlockSpec(memory_space=pltpu.HBM)


def scratch_of(rows):
    return [
        pltpu.VMEM((rows, rows), jnp.float32),
        pltpu.VMEM((rows, rows), jnp.float32),
        pltpu.VMEM((HEAD_SIZE + ONES_ROWS, rows), jnp.bfloat16),
        pltpu.VMEM((HEAD_SIZE + ONES_ROWS, rows), jnp.bfloat16),
    ]


def params_of(heads, rows, blocks, limit=VMEM_LIMIT):
    return dict(
        compiler_params=pltpu.CompilerParams(vmem_limit_bytes=limit),
        cost_estimate=pl.CostEstimate(
            flops=int(4 * heads * rows * rows * HEAD_SIZE * blocks),
            bytes_accessed=4 * heads * HEAD_SIZE * rows,
            transcendentals=int(heads * rows * rows * blocks),
        ),
    )


def local_attention(flags, own, received, pair, group, kv_heads, h):
    rows = own.shape[0]
    span = group * HEAD_SIZE
    stats = jax.ShapeDtypeStruct((2, group, rows), jnp.float32)

    def kernel(flags, own, received, *refs):
        at = slice(h * span, (h + 1) * span)
        local_kernel(flags, own.at[:, at], received.at[:, at], *refs)

    return pl.pallas_call(
        kernel,
        in_specs=[SMEM, VMEM, VMEM, VMEM],
        out_specs=[VMEM] * 5,
        out_shape=[
            jax.ShapeDtypeStruct((2, span, rows), jnp.bfloat16),
            stats,
            jax.ShapeDtypeStruct((2, span, rows), jnp.float32),
            stats,
            stats,
        ],
        scratch_shapes=scratch_of(rows),
        name=f"attend_local_{h}",
        **params_of(2 * group, rows, 1),
    )(flags, own, received, pair)


def window_attention(flags, qt, bound, pairs, state, group, name):
    rows = qt.shape[2]
    return pl.pallas_call(
        functools.partial(window_kernel, len(pairs)),
        in_specs=[SMEM] + [VMEM] * (5 + len(pairs)),
        out_specs=[VMEM] * 3,
        out_shape=[jax.ShapeDtypeStruct(a.shape, a.dtype) for a in state],
        scratch_shapes=scratch_of(rows),
        input_output_aliases={3 + len(pairs) + i: i for i in range(3)},
        name=name,
        **params_of(2 * group, rows, 2 * len(pairs)),
    )(flags, qt, bound, *pairs, *state)


def last_attention(flags, qt, bound, pairs, state, placed, width, group, kv_heads, h, name):
    rows = qt.shape[2]
    span = group * HEAD_SIZE
    return pl.pallas_call(
        functools.partial(last_kernel, len(pairs), kv_heads, h),
        in_specs=[SMEM] + [VMEM] * (5 + len(pairs)) + [HBM] * len(placed),
        out_specs=[HBM, HBM],
        out_shape=[
            jax.ShapeDtypeStruct((rows, width), jnp.bfloat16),
            jax.ShapeDtypeStruct((rows, span), jnp.bfloat16),
        ],
        scratch_shapes=[
            pltpu.VMEM((2, rows, span), jnp.bfloat16),
            pltpu.SemaphoreType.DMA((2,)),
            *scratch_of(rows),
        ],
        input_output_aliases={6 + len(pairs): 0} if placed else {},
        name=name,
        **params_of(2 * group, rows, 2 * len(pairs)),
    )(flags, qt, bound, *pairs, *state, *placed)


def cut_out(flags, queries):
    rows, width = queries.shape
    part = jax.ShapeDtypeStruct((rows, width // 2), queries.dtype)
    return pl.pallas_call(
        cut_kernel,
        in_specs=[SMEM, HBM],
        out_specs=[VMEM, VMEM],
        out_shape=[part, part],
        scratch_shapes=[pltpu.SemaphoreType.DMA((2,))],
        compiler_params=pltpu.CompilerParams(vmem_limit_bytes=CUT_VMEM_LIMIT),
        name="cut_queries",
    )(flags, queries)


def put_in(flags, pieces, out):
    return pl.pallas_call(
        place_kernel,
        in_specs=[SMEM] + [VMEM] * len(pieces) + [HBM],
        out_specs=HBM,
        out_shape=jax.ShapeDtypeStruct(out.shape, out.dtype),
        scratch_shapes=[pltpu.SemaphoreType.DMA((len(pieces),))],
        input_output_aliases={1 + len(pieces): 0},
        name="place_result",
    )(flags, *pieces, out)


def on_device(queries, keys, values, prefix_spans):
    rows, width = queries.shape
    length = lax.axis_size("ctx")
    kv_local = keys.shape[1] // HEAD_SIZE
    shared = kv_local % 2 == 1
    kv_heads, group = (kv_local, GROUP // 2) if shared else (kv_local // 2, GROUP)
    q_width, kv_width = width // 2, kv_heads * HEAD_SIZE

    position = lax.axis_index("ctx")
    core = position % 2
    lower = (position // 2) % 2 == 0
    swap = [(i, i ^ 1) for i in range(length)]
    across = [(i, i ^ 2) for i in range(length)]
    ahead = [(i, i + 4) for i in range(length - 4)]

    def halves(a):
        if shared:
            return a, a
        low, high = a[:, :kv_width], a[:, kv_width:]
        return jnp.where(core == 0, low, high), jnp.where(core == 0, high, low)

    k_mine, k_theirs = halves(keys)
    v_mine, v_theirs = halves(values)
    span_columns = jnp.broadcast_to(prefix_spans.astype(jnp.bfloat16), (rows, HEAD_SIZE))
    kv_sent = jnp.concatenate([k_theirs, v_theirs, span_columns], axis=1)
    core_flag = core[None].astype(jnp.int32)
    kv_got, q_flag = lax.optimization_barrier((moved(kv_sent, swap), core_flag))
    q_own, q_sent = cut_out(q_flag, queries)
    q_got = moved(q_sent, swap)

    def pair_of(h):
        at = head_rows(h)
        mine = jnp.concatenate([k_mine[:, at], v_mine[:, at]], axis=1)
        got = jnp.concatenate([kv_got[:, at], kv_got[:, kv_width:][:, at]], axis=1)
        return jnp.stack([jnp.where(core == 1, mine, got), jnp.where(core == 1, got, mine)])

    pairs = [pair_of(h) for h in range(kv_heads)]

    reach_own = jnp.minimum(prefix_spans[0], position)
    reach_other = jnp.minimum(kv_got[0, 2 * kv_width].astype(jnp.int32), position ^ 1)

    def counts(distance):
        first = 2 * distance - 1
        return [
            jnp.clip(reach_own - first - core + 1, 0, 2),
            jnp.clip(reach_other - first - (1 - core) + 1, 0, 2),
        ]

    near_flags = jnp.stack([core, *counts(1), *counts(2)]).astype(jnp.int32)
    far_flags = jnp.stack([core, *counts(3), *counts(4)]).astype(jnp.int32)

    def across_of(pair, second):
        return moved(jnp.where(lower, pair, second), across)

    heads = range(kv_heads)
    state, first, second, third, fourth = {}, {}, {}, {}, {}
    second[0] = moved(pairs[0], ahead)
    state[0] = local_attention(core_flag, q_own, q_got, pairs[0], group, kv_heads, 0)
    for h in heads[1:]:
        (second[h - 1], state[h - 1]) = lax.optimization_barrier((second[h - 1], state[h - 1]))
        second[h] = moved(pairs[h], ahead)
        first[h - 1] = across_of(pairs[h - 1], second[h - 1])
        state[h] = local_attention(core_flag, q_own, q_got, pairs[h], group, kv_heads, h)
    h = kv_heads - 1
    (second[h], first, state[h]) = lax.optimization_barrier((second[h], first, state[h]))
    first[h] = across_of(pairs[h], second[h])

    for h in heads:
        third[h] = moved(first[h], ahead)
        fourth[h] = moved(second[h], ahead)
        qt, bound, *old = state[h]
        new = window_attention(
            near_flags, qt, bound, [first[h], second[h]], old, group, f"attend_near_{h}"
        )
        state[h] = [qt, bound, *new]
        if h + 1 < kv_heads:
            (first[h + 1], state[h]) = lax.optimization_barrier((first[h + 1], state[h]))

    state, third, fourth = lax.optimization_barrier((state, third, fourth))
    out, returned = None, []
    for h in heads:
        qt, bound, *old = state[h]
        placed = [out] if h else []
        out, other = last_attention(
            far_flags, qt, bound, [third[h], fourth[h]], old, placed, width,
            group, kv_heads, h, f"attend_far_{h}",
        )
        returned.append(moved(other, swap))
    return put_in(core_flag, returned, out)


def solution(mesh):
    placed = (P("ctx", "tp"), P("ctx", "tp"), P("ctx", "tp"), P("ctx"))
    return jax.shard_map(
        on_device, mesh=mesh, in_specs=placed, out_specs=P("ctx", "tp"), check_vma=False
    )
```

```python
import functools
import math

import jax
import jax.numpy as jnp
from jax import lax
from jax.experimental import pallas as pl
from jax.experimental.pallas import tpu as pltpu
from jax.sharding import PartitionSpec as P

QUERY_HEAD_COUNT = 64
KEY_VALUE_HEADS = 8
HEAD_SIZE = 128
GROUP = QUERY_HEAD_COUNT // KEY_VALUE_HEADS
SCALE = math.log2(math.e) / math.sqrt(HEAD_SIZE)
EXPONENT_ROOM = 100.0
ONES_ROWS = 16
MIB = 1024 * 1024
VMEM_LIMIT = 10 * MIB
CUT_VMEM_LIMIT = 60 * MIB


def moved(shard, pairs):
    return lax.ppermute(shard, "ctx", pairs)


def head_rows(i):
    return slice(i * HEAD_SIZE, (i + 1) * HEAD_SIZE)


def column_max(s):
    return jnp.max(s, axis=0, keepdims=True)


def column_sum(s):
    return jnp.sum(s, axis=0, keepdims=True)


def dot(a, b):
    return jnp.dot(a, b, preferred_element_type=jnp.float32)


class Step:
    def __init__(self, refs, kv_ref, slot, head, at):
        self.qt_ref, self.acc_ref, self.m_ref, self.l_ref, s_refs, vt_refs = refs
        self.kv_ref, self.slot, self.head = kv_ref, slot, head
        self.s_ref, self.vt_ref = s_refs[at % 2], vt_refs[slot % 2]
        self.rows = self.qt_ref.shape[1]
        self.half = self.rows // 2

    def keys(self, c):
        return self.kv_ref[self.slot, c * self.half:(c + 1) * self.half, :HEAD_SIZE]

    def chunk(self, c):
        return slice(c * self.half, (c + 1) * self.half)

    @property
    def row(self):
        return slice(self.head, self.head + 1)


class DiagonalStep(Step):
    def scores(self, c):
        half = self.half
        lower = lax.broadcasted_iota(jnp.int32, (half, half), 0) <= lax.broadcasted_iota(
            jnp.int32, (half, half), 1
        )
        qt = self.qt_ref[head_rows(self.head), :]
        if c == 0:
            near = jnp.where(lower, dot(self.keys(0), qt[:, :half]), -jnp.inf)
            over = dot(self.keys(0), qt[:, half:])
            self.s_ref[:half, :half] = near
            self.s_ref[:half, half:] = over
            return jnp.concatenate([column_max(near), column_max(over)], axis=1)
        far = jnp.where(lower, dot(self.keys(1), qt[:, half:]), -jnp.inf)
        self.s_ref[half:, half:] = far
        return jnp.concatenate([jnp.full((1, half), -jnp.inf, jnp.float32), column_max(far)], axis=1)

    def start(self, top):
        self.m = top * SCALE

    def weigh(self, c):
        half = self.half
        if c == 0:
            p = jnp.exp2(self.s_ref[:half, :] * SCALE - self.m)
            self.l0 = column_sum(p)
            self.p0 = p.astype(jnp.bfloat16)
        else:
            p = jnp.exp2(self.s_ref[half:, half:] * SCALE - self.m[:, half:])
            self.l1 = column_sum(p)
            self.p1 = p.astype(jnp.bfloat16)

    def finish(self):
        half = self.half
        at = head_rows(self.head)
        self.acc_ref[at, :half] = dot(self.vt_ref[:HEAD_SIZE, :half], self.p0[:, :half])
        self.acc_ref[at, half:] = dot(
            self.vt_ref[:HEAD_SIZE, :], jnp.concatenate([self.p0[:, half:], self.p1], axis=0)
        )
        self.m_ref[self.row, :] = self.m
        self.l_ref[self.row, :half] = self.l0[:, :half]
        self.l_ref[self.row, half:] = self.l0[:, half:] + self.l1


def run_diagonal(refs, kv_ref, slot):
    refs[5][slot % 2][:HEAD_SIZE, :] = kv_ref[slot, :, HEAD_SIZE:].T
    steps = [DiagonalStep(refs, kv_ref, slot, i, i) for i in range(refs[2].shape[0])]
    top = jnp.maximum(steps[0].scores(0), steps[0].scores(1))
    for now, after in zip(steps, steps[1:] + [None]):
        now.start(top)
        tops = []
        for c in range(2):
            if after is not None:
                tops.append(after.scores(c))
            now.weigh(c)
        now.finish()
        if tops:
            top = jnp.maximum(*tops)


def run_bounded(refs, kv_ref, slots):
    qt_ref, acc_ref, m_ref, l_ref, _, vt_refs = refs
    heads, rows = m_ref.shape
    half = rows // 2

    def weights(slot, i):
        qt = qt_ref[head_rows(i), :]
        m = m_ref[i:i + 1, :]
        parts = []
        for c in range(2):
            s = dot(kv_ref[slot, c * half:(c + 1) * half, :HEAD_SIZE], qt)
            parts.append(jnp.exp2(s * SCALE - m).astype(jnp.bfloat16))
        return jnp.concatenate(parts, axis=0)

    def add(slot, i, w):
        o = dot(vt_refs[slot % 2][...], w)
        acc_ref[head_rows(i), :] += o[:HEAD_SIZE, :]
        l_ref[i:i + 1, :] += o[HEAD_SIZE:HEAD_SIZE + 1, :]

    waiting = None
    for slot in slots:
        vt_refs[slot % 2][:HEAD_SIZE, :] = kv_ref[slot, :, HEAD_SIZE:].T
        for i in range(heads):
            w = weights(slot, i)
            if waiting is not None:
                add(*waiting)
            waiting = (slot, i, w)
    add(*waiting)


def run_exact(refs, kv_ref, slots):
    qt_ref, acc_ref, m_ref, l_ref, _, vt_refs = refs
    for slot in slots:
        vt_refs[slot % 2][:HEAD_SIZE, :] = kv_ref[slot, :, HEAD_SIZE:].T

        def head(i, carry, slot=slot):
            at = pl.ds(pl.multiple_of(i * HEAD_SIZE, HEAD_SIZE), HEAD_SIZE)
            row = pl.ds(i, 1)
            s = dot(kv_ref[slot, :, :HEAD_SIZE], qt_ref[at, :]) * SCALE
            m_old = m_ref[row, :]
            m = jnp.maximum(m_old, column_max(s))
            correct = jnp.exp2(m_old - m)
            o = dot(vt_refs[slot % 2][...], jnp.exp2(s - m).astype(jnp.bfloat16))
            acc_ref[at, :] = acc_ref[at, :] * correct + o[:HEAD_SIZE, :]
            l_ref[row, :] = l_ref[row, :] * correct + o[HEAD_SIZE:HEAD_SIZE + 1, :]
            m_ref[row, :] = m
            return carry

        lax.fori_loop(0, m_ref.shape[0], head, 0)


def run_whole(refs, bound_ref, kv_ref, slots):
    longest = 0.0
    for slot in slots:
        k = kv_ref[slot, :, :HEAD_SIZE].astype(jnp.float32)
        longest = jnp.maximum(longest, jnp.max(jnp.sum(k * k, axis=1, keepdims=True)))
    longest = jnp.sqrt(jnp.full((1, 1), longest, jnp.float32))
    bounded = jnp.max(bound_ref[...] * longest - refs[2][...]) <= EXPONENT_ROOM
    pl.when(bounded)(lambda: run_bounded(refs, kv_ref, slots))
    pl.when(jnp.logical_not(bounded))(lambda: run_exact(refs, kv_ref, slots))


def fill_ones(vt_refs):
    for vt_ref in vt_refs:
        vt_ref[HEAD_SIZE:, :] = jnp.ones((ONES_ROWS, vt_ref.shape[1]), jnp.bfloat16)


def refs_for(work, b):
    qt_ref, acc_ref, m_ref, l_ref, *rest = work
    return (qt_ref.at[b], acc_ref.at[b], m_ref.at[b], l_ref.at[b], rest[:2], rest[2:])


def turn(q_ref, qt_ref, bound_ref):
    for i in range(q_ref.shape[1] // HEAD_SIZE):
        qt = q_ref[:, head_rows(i)].T
        qt_ref[head_rows(i), :] = qt
        wide = qt.astype(jnp.float32)
        bound_ref[i:i + 1, :] = jnp.sqrt(column_sum(wide * wide)) * (SCALE * 1.01)


def own_kernel(kv_heads, shared, flags, queries, keys, values, *refs):
    states, (q_buf, arrived, kv_buf, *scratch) = refs[:5 * kv_heads], refs[5 * kv_heads:]
    core = flags[0]
    span = q_buf.shape[2]
    copies = []
    for h in range(kv_heads):
        at = pl.multiple_of((core * kv_heads + h) * span, span)
        copies.append(pltpu.make_async_copy(queries.at[:, pl.ds(at, span)], q_buf.at[h], arrived.at[h]))
        copies[h].start()
    for h in range(kv_heads):
        head = h if shared else core * kv_heads + h
        at = pl.ds(pl.multiple_of(head * HEAD_SIZE, HEAD_SIZE), HEAD_SIZE)
        kv_buf[0, :, :HEAD_SIZE] = keys[:, at]
        kv_buf[0, :, HEAD_SIZE:] = values[:, at]
        qt_ref, bound_ref, acc_ref, m_ref, l_ref = [ref.at[0] for ref in states[5 * h:5 * h + 5]]
        copies[h].wait()
        turn(q_buf.at[h], qt_ref, bound_ref)
        run_diagonal((qt_ref, acc_ref, m_ref, l_ref, scratch[:2], scratch[2:]), kv_buf, 0)


def add_other(h, flags, received, kv_ref, bound_ref, work):
    core = flags[0]
    span = work[0].shape[1]
    turn(received.at[:, h * span:(h + 1) * span], work[0].at[1], bound_ref.at[1])
    pl.when(core == 0)(lambda: run_diagonal(refs_for(work, 1), kv_ref, 0))
    pl.when(core == 1)(lambda: run_diagonal(refs_for(work, 1), kv_ref, 1))
    odd = 1 - core
    run_whole(refs_for(work, odd), bound_ref.at[odd], kv_ref, [1])


def add_window(flags, work, bound_ref, kv_ref, pieces, b):
    refs = refs_for(work, b)
    for distance, slots in pieces:
        count = flags[2 * distance - 1 + b]
        for most in range(1, len(slots) + 1):
            add = functools.partial(run_whole, refs, bound_ref.at[b], kv_ref, slots[:most])
            pl.when(count == most)(add)
    return refs


OTHER, SECOND, FIRST, BEYOND = range(4)
PIECES = {SECOND: [(2, [0, 1])], FIRST: [(1, [0, 1])], BEYOND: [(3, [0, 1]), (4, [2])]}
WRITTEN = {OTHER: range(5), SECOND: range(2, 5), FIRST: range(2, 5), BEYOND: ()}


def phase_kernel(jobs, kv_heads, placed, flags, *refs):
    refs = list(refs)
    take = lambda n: [refs.pop(0) for _ in range(n)]
    received = take(1)[0] if jobs[-1][1] == OTHER else None
    inputs = [take(6) for _ in jobs]
    take(placed)
    outputs = [take(len(WRITTEN[stage])) for _, stage in jobs]
    if jobs[0][1] == BEYOND:
        out, other, stage_buf, sent = take(4)
    scratch = refs
    fill_ones(scratch[2:])
    for (h, stage), (kv_ref, *state), new in zip(jobs, inputs, outputs):
        for at, ref in zip(WRITTEN[stage], new):
            state[at] = ref
        qt_ref, bound_ref, acc_ref, m_ref, l_ref = state
        work = (qt_ref, acc_ref, m_ref, l_ref, *scratch)
        if stage == OTHER:
            add_other(h, flags, received, kv_ref, bound_ref, work)
            continue

        def block(b, carry, stage=stage, work=work, bound_ref=bound_ref, kv_ref=kv_ref):
            _, acc_ref, _, l_ref, *_ = add_window(flags, work, bound_ref, kv_ref, PIECES[stage], b)
            if stage == BEYOND:
                for i in range(stage_buf.shape[2] // HEAD_SIZE):
                    result = acc_ref[head_rows(i), :] / l_ref[i:i + 1, :]
                    stage_buf[b, :, head_rows(i)] = result.T.astype(stage_buf.dtype)
            return carry

        lax.fori_loop(0, 2, block, 0)
        if stage == BEYOND:
            span = stage_buf.shape[2]
            own_at = pl.multiple_of((flags[0] * kv_heads + h) * span, span)
            copies = [
                pltpu.make_async_copy(stage_buf.at[0], out.at[:, pl.ds(own_at, span)], sent.at[0]),
                pltpu.make_async_copy(stage_buf.at[1], other, sent.at[1]),
            ]
            for copy in copies:
                copy.start()
    if jobs[0][1] == BEYOND:
        for copy in copies:
            copy.wait()


def cut_kernel(flags, queries, out, done):
    width = out.shape[1]
    at = pl.multiple_of((1 - flags[0]) * width, width)
    copy = pltpu.make_async_copy(queries.at[:, pl.ds(at, width)], out, done.at[0])
    copy.start()
    copy.wait()


def place_kernel(flags, *refs):
    *pieces, _, out, done = refs
    width = pieces[0].shape[1]
    copies = []
    for i, piece in enumerate(pieces):
        at = pl.multiple_of(((1 - flags[0]) * len(pieces) + i) * width, width)
        copies.append(pltpu.make_async_copy(piece, out.at[:, pl.ds(at, width)], done.at[i]))
    for copy in copies:
        copy.start()
    for copy in copies:
        copy.wait()


SMEM = pl.BlockSpec(memory_space=pltpu.SMEM)
VMEM = pl.BlockSpec(memory_space=pltpu.VMEM)
HBM = pl.BlockSpec(memory_space=pltpu.HBM)


def scratch_of(rows):
    return [
        pltpu.VMEM((rows, rows), jnp.float32),
        pltpu.VMEM((rows, rows), jnp.float32),
        pltpu.VMEM((HEAD_SIZE + ONES_ROWS, rows), jnp.bfloat16),
        pltpu.VMEM((HEAD_SIZE + ONES_ROWS, rows), jnp.bfloat16),
    ]


def params_of(heads, rows, blocks, limit=VMEM_LIMIT):
    return dict(
        compiler_params=pltpu.CompilerParams(vmem_limit_bytes=limit),
        cost_estimate=pl.CostEstimate(
            flops=int(heads * rows * HEAD_SIZE * blocks),
            bytes_accessed=heads * rows,
            transcendentals=0,
        ),
    )


def state_shapes(group, rows):
    span = group * HEAD_SIZE
    stats = jax.ShapeDtypeStruct((2, group, rows), jnp.float32)
    return [
        jax.ShapeDtypeStruct((2, span, rows), jnp.bfloat16),
        stats,
        jax.ShapeDtypeStruct((2, span, rows), jnp.float32),
        stats,
        stats,
    ]


def own_attention(flags, queries, keys, values, group, kv_heads, shared):
    rows = queries.shape[0]
    span = group * HEAD_SIZE
    states = pl.pallas_call(
        functools.partial(own_kernel, kv_heads, shared),
        in_specs=[SMEM, HBM, VMEM, VMEM],
        out_specs=[VMEM] * (5 * kv_heads),
        out_shape=state_shapes(group, rows) * kv_heads,
        scratch_shapes=[
            pltpu.VMEM((kv_heads, rows, span), jnp.bfloat16),
            pltpu.SemaphoreType.DMA((kv_heads,)),
            pltpu.VMEM((1, rows, 2 * HEAD_SIZE), jnp.bfloat16),
            *scratch_of(rows),
        ],
        name="attend_own",
        **params_of(kv_heads * group, rows, 1),
    )(flags, queries, keys, values)
    return [states[5 * h:5 * h + 5] for h in range(kv_heads)]


def phase(jobs, flags, received, kvs, states, placed, width, group, kv_heads):
    rows = states[0][0].shape[2]
    span = group * HEAD_SIZE
    ends, opens = jobs[0][1] == BEYOND, jobs[-1][1] == OTHER
    args, in_specs = [flags], [SMEM]
    if opens:
        args, in_specs = args + [received], in_specs + [VMEM]
    out_shape, out_specs, aliases, where = [], [], {}, []
    for (h, stage), kv in zip(jobs, kvs):
        for at in WRITTEN[stage]:
            aliases[len(args) + 1 + at] = len(out_shape)
            where.append((h, at))
            out_shape.append(state_shapes(group, rows)[at])
            out_specs.append(VMEM)
        args += [kv, *states[h]]
        in_specs += [VMEM] * 6
    scratch = scratch_of(rows)
    if ends:
        if placed is not None:
            aliases[len(args)] = len(out_shape)
            args, in_specs = args + [placed], in_specs + [HBM]
        out_shape += [
            jax.ShapeDtypeStruct((rows, width), jnp.bfloat16),
            jax.ShapeDtypeStruct((rows, span), jnp.bfloat16),
        ]
        out_specs += [HBM, HBM]
        scratch = [
            pltpu.VMEM((2, rows, span), jnp.bfloat16),
            pltpu.SemaphoreType.DMA((2,)),
            *scratch,
        ]
    results = pl.pallas_call(
        functools.partial(phase_kernel, jobs, kv_heads, int(placed is not None and ends)),
        in_specs=in_specs,
        out_specs=out_specs,
        out_shape=out_shape,
        scratch_shapes=scratch,
        input_output_aliases=aliases,
        name="attend" + "".join(f"_{'other second first beyond'.split()[k]}{h}" for h, k in jobs),
        **params_of(2 * group, rows, 1),
    )(*args)
    for (h, at), result in zip(where, results):
        states[h][at] = result
    return results[len(where):]


def cut_out(flags, queries):
    rows, width = queries.shape
    return pl.pallas_call(
        cut_kernel,
        in_specs=[SMEM, HBM],
        out_specs=VMEM,
        out_shape=jax.ShapeDtypeStruct((rows, width // 2), queries.dtype),
        scratch_shapes=[pltpu.SemaphoreType.DMA((1,))],
        compiler_params=pltpu.CompilerParams(vmem_limit_bytes=CUT_VMEM_LIMIT),
        name="cut_queries",
    )(flags, queries)


def put_in(flags, pieces, out):
    return pl.pallas_call(
        place_kernel,
        in_specs=[SMEM] + [VMEM] * len(pieces) + [HBM],
        out_specs=HBM,
        out_shape=jax.ShapeDtypeStruct(out.shape, out.dtype),
        scratch_shapes=[pltpu.SemaphoreType.DMA((len(pieces),))],
        input_output_aliases={1 + len(pieces): 0},
        compiler_params=pltpu.CompilerParams(vmem_limit_bytes=4 * MIB),
        name="place_result",
    )(flags, *pieces, out)


def on_device(queries, keys, values, prefix_spans):
    rows, width = queries.shape
    length = lax.axis_size("ctx")
    kv_local = keys.shape[1] // HEAD_SIZE
    shared = kv_local % 2 == 1
    kv_heads, group = (kv_local, GROUP // 2) if shared else (kv_local // 2, GROUP)
    q_width, kv_width = width // 2, kv_heads * HEAD_SIZE

    position = lax.axis_index("ctx")
    core = position % 2
    lower = (position // 2) % 2 == 0
    swap = [(i, i ^ 1) for i in range(length)]
    across = [(i, i ^ 2) for i in range(length)]
    ahead = [(i, i + 4) for i in range(length - 4)]

    def halves(a):
        if shared:
            return a, a
        low, high = a[:, :kv_width], a[:, kv_width:]
        return jnp.where(core == 0, low, high), jnp.where(core == 0, high, low)

    k_mine, k_theirs = halves(keys)
    v_mine, v_theirs = halves(values)
    span_columns = jnp.broadcast_to(prefix_spans.astype(jnp.bfloat16), (rows, HEAD_SIZE))
    core_flag = core[None].astype(jnp.int32)
    kv_sent = jnp.concatenate([k_theirs, v_theirs, span_columns], axis=1)
    kv_sent, cut_flag = lax.optimization_barrier((kv_sent, core_flag))
    kv_got = moved(kv_sent, swap)
    q_got = moved(cut_out(cut_flag, queries), swap)
    kv_got, own_flag = lax.optimization_barrier((kv_got, core_flag))

    def pair_of(h):
        at = head_rows(h)
        mine = jnp.concatenate([k_mine[:, at], v_mine[:, at]], axis=1)
        got = jnp.concatenate([kv_got[:, at], kv_got[:, kv_width:][:, at]], axis=1)
        return jnp.stack([jnp.where(core == 1, mine, got), jnp.where(core == 1, got, mine)])

    pairs = [pair_of(h) for h in range(kv_heads)]

    reach_own = jnp.minimum(prefix_spans[0], position)
    reach_other = jnp.minimum(kv_got[0, 2 * kv_width].astype(jnp.int32), position ^ 1)

    def counts(distance):
        first = 2 * distance - 1
        return [
            jnp.clip(reach_own - first - core + 1, 0, 2),
            jnp.clip(reach_other - first - (1 - core) + 1, 0, 2),
        ]

    flags = jnp.stack([core, *[n for d in range(1, 5) for n in counts(d)]]).astype(jnp.int32)

    def across_of(pair, second):
        return moved(jnp.where(lower, pair, second), across)

    heads = range(kv_heads)
    second = [moved(pairs[h], ahead) for h in heads]
    states = own_attention(own_flag, queries, keys, values, group, kv_heads, shared)
    states = [list(state) for state in states]
    first, beyond, out, returned = {}, {}, None, []
    for t in range(kv_heads + 3):
        jobs = [(h, t - h) for h in heads if 0 <= t - h <= BEYOND]
        arrived = [[pairs, second, first, beyond][stage][h] for h, stage in jobs]
        if t > 0:
            arrived, states = lax.optimization_barrier((arrived, states))
        for (h, stage), kv in zip(jobs, arrived):
            if stage == SECOND:
                second[h] = kv
                first[h] = across_of(pairs[h], kv)
            if stage == FIRST:
                beyond[h] = moved(jnp.concatenate([kv, second[h][:1]]), ahead)
        done = phase(jobs, flags, q_got, arrived, states, out, width, group, kv_heads)
        if done:
            out = done[0]
            returned.append(moved(done[1], swap))
    return put_in(core_flag, returned, out)


def solution(mesh):
    placed = (P("ctx", "tp"), P("ctx", "tp"), P("ctx", "tp"), P("ctx"))
    return jax.shard_map(
        on_device, mesh=mesh, in_specs=placed, out_specs=P("ctx", "tp"), check_vma=False
    )
```

```python
import functools
import math

import jax
import jax.numpy as jnp
from jax import lax
from jax.experimental import pallas as pl
from jax.experimental.pallas import tpu as pltpu
from jax.sharding import PartitionSpec as P

QUERY_HEAD_COUNT = 64
KEY_VALUE_HEADS = 8
HEAD_SIZE = 128
GROUP = QUERY_HEAD_COUNT // KEY_VALUE_HEADS
SCALE = math.log2(math.e) / math.sqrt(HEAD_SIZE)
EXPONENT_ROOM = 100.0
ONES_ROWS = 16
MIB = 1024 * 1024
VMEM_LIMIT = 10 * MIB
CUT_VMEM_LIMIT = 60 * MIB
OWN_VMEM_LIMIT = 40 * MIB


def moved(shard, pairs):
    return lax.ppermute(shard, "ctx", pairs)


def head_rows(i):
    return slice(i * HEAD_SIZE, (i + 1) * HEAD_SIZE)


def column_max(s):
    return jnp.max(s, axis=0, keepdims=True)


def column_sum(s):
    return jnp.sum(s, axis=0, keepdims=True)


def dot(a, b):
    return jnp.dot(a, b, preferred_element_type=jnp.float32)


class Step:
    def __init__(self, refs, kv_ref, slot, head, at):
        self.qt_ref, self.acc_ref, self.m_ref, self.l_ref, s_refs, vt_refs = refs
        self.kv_ref, self.slot, self.head = kv_ref, slot, head
        self.s_ref, self.vt_ref = s_refs[at % 2], vt_refs[slot % 2]
        self.rows = self.qt_ref.shape[1]
        self.half = self.rows // 2

    def keys(self, c):
        return self.kv_ref[self.slot, c * self.half:(c + 1) * self.half, :HEAD_SIZE]

    def chunk(self, c):
        return slice(c * self.half, (c + 1) * self.half)

    @property
    def row(self):
        return slice(self.head, self.head + 1)


class DiagonalStep(Step):
    def scores(self, c):
        half = self.half
        lower = lax.broadcasted_iota(jnp.int32, (half, half), 0) <= lax.broadcasted_iota(
            jnp.int32, (half, half), 1
        )
        qt = self.qt_ref[head_rows(self.head), :]
        if c == 0:
            near = jnp.where(lower, dot(self.keys(0), qt[:, :half]), -jnp.inf)
            over = dot(self.keys(0), qt[:, half:])
            self.s_ref[:half, :half] = near
            self.s_ref[:half, half:] = over
            return jnp.concatenate([column_max(near), column_max(over)], axis=1)
        far = jnp.where(lower, dot(self.keys(1), qt[:, half:]), -jnp.inf)
        self.s_ref[half:, half:] = far
        return jnp.concatenate([jnp.full((1, half), -jnp.inf, jnp.float32), column_max(far)], axis=1)

    def start(self, top):
        self.m = top * SCALE

    def weigh(self, c):
        half = self.half
        if c == 0:
            p = jnp.exp2(self.s_ref[:half, :] * SCALE - self.m)
            self.l0 = column_sum(p)
            self.p0 = p.astype(jnp.bfloat16)
        else:
            p = jnp.exp2(self.s_ref[half:, half:] * SCALE - self.m[:, half:])
            self.l1 = column_sum(p)
            self.p1 = p.astype(jnp.bfloat16)

    def finish(self):
        half = self.half
        at = head_rows(self.head)
        self.acc_ref[at, :half] = dot(self.vt_ref[:HEAD_SIZE, :half], self.p0[:, :half])
        self.acc_ref[at, half:] = dot(
            self.vt_ref[:HEAD_SIZE, :], jnp.concatenate([self.p0[:, half:], self.p1], axis=0)
        )
        self.m_ref[self.row, :] = self.m
        self.l_ref[self.row, :half] = self.l0[:, :half]
        self.l_ref[self.row, half:] = self.l0[:, half:] + self.l1


def run_diagonal(refs, kv_ref, slot):
    refs[5][slot % 2][:HEAD_SIZE, :] = kv_ref[slot, :, HEAD_SIZE:].T
    steps = [DiagonalStep(refs, kv_ref, slot, i, i) for i in range(refs[2].shape[0])]
    top = jnp.maximum(steps[0].scores(0), steps[0].scores(1))
    for now, after in zip(steps, steps[1:] + [None]):
        now.start(top)
        tops = []
        for c in range(2):
            if after is not None:
                tops.append(after.scores(c))
            now.weigh(c)
        now.finish()
        if tops:
            top = jnp.maximum(*tops)


def run_bounded(refs, kv_ref, slots):
    qt_ref, acc_ref, m_ref, l_ref, _, vt_refs = refs
    heads, rows = m_ref.shape
    half = rows // 2

    def weights(slot, i):
        qt = qt_ref[head_rows(i), :]
        m = m_ref[i:i + 1, :]
        parts = []
        for c in range(2):
            s = dot(kv_ref[slot, c * half:(c + 1) * half, :HEAD_SIZE], qt)
            parts.append(jnp.exp2(s * SCALE - m).astype(jnp.bfloat16))
        return jnp.concatenate(parts, axis=0)

    def add(slot, i, w):
        o = dot(vt_refs[slot % 2][...], w)
        acc_ref[head_rows(i), :] += o[:HEAD_SIZE, :]
        l_ref[i:i + 1, :] += o[HEAD_SIZE:HEAD_SIZE + 1, :]

    waiting = None
    for slot in slots:
        vt_refs[slot % 2][:HEAD_SIZE, :] = kv_ref[slot, :, HEAD_SIZE:].T
        for i in range(heads):
            w = weights(slot, i)
            if waiting is not None:
                add(*waiting)
            waiting = (slot, i, w)
    add(*waiting)


def run_exact(refs, kv_ref, slots):
    qt_ref, acc_ref, m_ref, l_ref, _, vt_refs = refs
    for slot in slots:
        vt_refs[slot % 2][:HEAD_SIZE, :] = kv_ref[slot, :, HEAD_SIZE:].T

        def head(i, carry, slot=slot):
            at = pl.ds(pl.multiple_of(i * HEAD_SIZE, HEAD_SIZE), HEAD_SIZE)
            row = pl.ds(i, 1)
            s = dot(kv_ref[slot, :, :HEAD_SIZE], qt_ref[at, :]) * SCALE
            m_old = m_ref[row, :]
            m = jnp.maximum(m_old, column_max(s))
            correct = jnp.exp2(m_old - m)
            o = dot(vt_refs[slot % 2][...], jnp.exp2(s - m).astype(jnp.bfloat16))
            acc_ref[at, :] = acc_ref[at, :] * correct + o[:HEAD_SIZE, :]
            l_ref[row, :] = l_ref[row, :] * correct + o[HEAD_SIZE:HEAD_SIZE + 1, :]
            m_ref[row, :] = m
            return carry

        lax.fori_loop(0, m_ref.shape[0], head, 0)


def run_whole(refs, bound_ref, kv_ref, slots):
    longest = 0.0
    for slot in slots:
        k = kv_ref[slot, :, :HEAD_SIZE].astype(jnp.float32)
        longest = jnp.maximum(longest, jnp.max(jnp.sum(k * k, axis=1, keepdims=True)))
    longest = jnp.sqrt(jnp.full((1, 1), longest, jnp.float32))
    bounded = jnp.max(bound_ref[...] * longest - refs[2][...]) <= EXPONENT_ROOM
    pl.when(bounded)(lambda: run_bounded(refs, kv_ref, slots))
    pl.when(jnp.logical_not(bounded))(lambda: run_exact(refs, kv_ref, slots))


def fill_ones(vt_refs):
    for vt_ref in vt_refs:
        vt_ref[HEAD_SIZE:, :] = jnp.ones((ONES_ROWS, vt_ref.shape[1]), jnp.bfloat16)


def refs_for(work, b):
    qt_ref, acc_ref, m_ref, l_ref, *rest = work
    return (qt_ref.at[b], acc_ref.at[b], m_ref.at[b], l_ref.at[b], rest[:2], rest[2:])


def turn(q_ref, qt_ref, bound_ref):
    for i in range(q_ref.shape[1] // HEAD_SIZE):
        qt = q_ref[:, head_rows(i)].T
        qt_ref[head_rows(i), :] = qt
        wide = qt.astype(jnp.float32)
        bound_ref[i:i + 1, :] = jnp.sqrt(column_sum(wide * wide)) * (SCALE * 1.01)


def own_kernel(kv_heads, shared, flags, queries, keys, values, *refs):
    states, (q_buf, arrived, kv_buf, *scratch) = refs[:5 * kv_heads], refs[5 * kv_heads:]
    core = flags[0]
    span = q_buf.shape[2]
    copies = []
    for h in range(kv_heads):
        at = pl.multiple_of((core * kv_heads + h) * span, span)
        head = h if shared else core * kv_heads + h
        kv_at = pl.ds(pl.multiple_of(head * HEAD_SIZE, HEAD_SIZE), HEAD_SIZE)
        moves = [
            (queries.at[:, pl.ds(at, span)], q_buf.at[h]),
            (keys.at[:, kv_at], kv_buf.at[h, :, :HEAD_SIZE]),
            (values.at[:, kv_at], kv_buf.at[h, :, HEAD_SIZE:]),
        ]
        copies.append(
            [pltpu.make_async_copy(*move, arrived.at[3 * h + i]) for i, move in enumerate(moves)]
        )
        for copy in copies[h]:
            copy.start()
    for h in range(kv_heads):
        qt_ref, bound_ref, acc_ref, m_ref, l_ref = [ref.at[0] for ref in states[5 * h:5 * h + 5]]
        for copy in copies[h]:
            copy.wait()
        turn(q_buf.at[h], qt_ref, bound_ref)
        run_diagonal((qt_ref, acc_ref, m_ref, l_ref, scratch[:2], scratch[2:]), kv_buf, h)


def pair_kernel(kv_heads, shared, flags, keys, values, got, *refs):
    *pairs, span = refs
    core = flags[0]
    for h, pair in enumerate(pairs):
        at = head_rows(h)
        head = h if shared else core * kv_heads + h
        kv_at = pl.ds(pl.multiple_of(head * HEAD_SIZE, HEAD_SIZE), HEAD_SIZE)
        mine = 1 - core
        pair[mine, :, :HEAD_SIZE] = keys[:, kv_at]
        pair[mine, :, HEAD_SIZE:] = values[:, kv_at]
        pair[core, :, :HEAD_SIZE] = got[:, at]
        pair[core, :, HEAD_SIZE:] = got[:, head_rows(kv_heads + h)]
    last = got[:16, head_rows(2 * kv_heads)].astype(jnp.float32)
    span[0] = jnp.max(last).astype(jnp.int32)


def add_other(h, flags, received, kv_ref, bound_ref, work):
    core = flags[0]
    span = work[0].shape[1]
    turn(received.at[:, h * span:(h + 1) * span], work[0].at[1], bound_ref.at[1])
    pl.when(core == 0)(lambda: run_diagonal(refs_for(work, 1), kv_ref, 0))
    pl.when(core == 1)(lambda: run_diagonal(refs_for(work, 1), kv_ref, 1))
    odd = 1 - core
    run_whole(refs_for(work, odd), bound_ref.at[odd], kv_ref, [1])


def add_window(flags, work, bound_ref, kv_ref, pieces, b):
    refs = refs_for(work, b)
    for distance, slots in pieces:
        count = flags[2 * distance - 1 + b]
        for most in range(1, len(slots) + 1):
            add = functools.partial(run_whole, refs, bound_ref.at[b], kv_ref, slots[:most])
            pl.when(count == most)(add)
    return refs


OTHER, SECOND, FIRST, BEYOND = range(4)
PIECES = {SECOND: [(2, [0, 1])], FIRST: [(1, [0, 1])], BEYOND: [(3, [0, 1]), (4, [2])]}
WRITTEN = {OTHER: range(5), SECOND: range(2, 5), FIRST: range(2, 5), BEYOND: ()}


def phase_kernel(jobs, kv_heads, placed, flags, *refs):
    refs = list(refs)
    take = lambda n: [refs.pop(0) for _ in range(n)]
    received = take(1)[0] if jobs[-1][1] == OTHER else None
    inputs = [take(6) for _ in jobs]
    take(placed)
    outputs = [take(len(WRITTEN[stage])) for _, stage in jobs]
    if jobs[0][1] == BEYOND:
        out, other, stage_buf, sent = take(4)
    scratch = refs
    fill_ones(scratch[2:])
    for (h, stage), (kv_ref, *state), new in zip(jobs, inputs, outputs):
        for at, ref in zip(WRITTEN[stage], new):
            state[at] = ref
        qt_ref, bound_ref, acc_ref, m_ref, l_ref = state
        work = (qt_ref, acc_ref, m_ref, l_ref, *scratch)
        if stage == OTHER:
            add_other(h, flags, received, kv_ref, bound_ref, work)
            continue

        def block(b, carry, stage=stage, work=work, bound_ref=bound_ref, kv_ref=kv_ref):
            _, acc_ref, _, l_ref, *_ = add_window(flags, work, bound_ref, kv_ref, PIECES[stage], b)
            if stage == BEYOND:
                for i in range(stage_buf.shape[2] // HEAD_SIZE):
                    result = acc_ref[head_rows(i), :] / l_ref[i:i + 1, :]
                    stage_buf[b, :, head_rows(i)] = result.T.astype(stage_buf.dtype)
            return carry

        lax.fori_loop(0, 2, block, 0)
        if stage == BEYOND:
            span = stage_buf.shape[2]
            own_at = pl.multiple_of((flags[0] * kv_heads + h) * span, span)
            copies = [
                pltpu.make_async_copy(stage_buf.at[0], out.at[:, pl.ds(own_at, span)], sent.at[0]),
                pltpu.make_async_copy(stage_buf.at[1], other, sent.at[1]),
            ]
            for copy in copies:
                copy.start()
    if jobs[0][1] == BEYOND:
        for copy in copies:
            copy.wait()


def cut_kernel(flags, queries, out, done):
    width = out.shape[1]
    at = pl.multiple_of((1 - flags[0]) * width, width)
    copy = pltpu.make_async_copy(queries.at[:, pl.ds(at, width)], out, done.at[0])
    copy.start()
    copy.wait()


def place_kernel(flags, *refs):
    *pieces, _, out, done = refs
    width = pieces[0].shape[1]
    copies = []
    for i, piece in enumerate(pieces):
        at = pl.multiple_of(((1 - flags[0]) * len(pieces) + i) * width, width)
        copies.append(pltpu.make_async_copy(piece, out.at[:, pl.ds(at, width)], done.at[i]))
    for copy in copies:
        copy.start()
    for copy in copies:
        copy.wait()


SMEM = pl.BlockSpec(memory_space=pltpu.SMEM)
VMEM = pl.BlockSpec(memory_space=pltpu.VMEM)
HBM = pl.BlockSpec(memory_space=pltpu.HBM)


def scratch_of(rows):
    return [
        pltpu.VMEM((rows, rows), jnp.float32),
        pltpu.VMEM((rows, rows), jnp.float32),
        pltpu.VMEM((HEAD_SIZE + ONES_ROWS, rows), jnp.bfloat16),
        pltpu.VMEM((HEAD_SIZE + ONES_ROWS, rows), jnp.bfloat16),
    ]


def params_of(heads, rows, blocks, limit=VMEM_LIMIT):
    return dict(
        compiler_params=pltpu.CompilerParams(vmem_limit_bytes=limit),
        cost_estimate=pl.CostEstimate(
            flops=int(heads * rows * HEAD_SIZE * blocks),
            bytes_accessed=heads * rows,
            transcendentals=0,
        ),
    )


def state_shapes(group, rows):
    span = group * HEAD_SIZE
    stats = jax.ShapeDtypeStruct((2, group, rows), jnp.float32)
    return [
        jax.ShapeDtypeStruct((2, span, rows), jnp.bfloat16),
        stats,
        jax.ShapeDtypeStruct((2, span, rows), jnp.float32),
        stats,
        stats,
    ]


def own_attention(flags, queries, keys, values, group, kv_heads, shared):
    rows = queries.shape[0]
    span = group * HEAD_SIZE
    states = pl.pallas_call(
        functools.partial(own_kernel, kv_heads, shared),
        in_specs=[SMEM, HBM, HBM, HBM],
        out_specs=[VMEM] * (5 * kv_heads),
        out_shape=state_shapes(group, rows) * kv_heads,
        scratch_shapes=[
            pltpu.VMEM((kv_heads, rows, span), jnp.bfloat16),
            pltpu.SemaphoreType.DMA((3 * kv_heads,)),
            pltpu.VMEM((kv_heads, rows, 2 * HEAD_SIZE), jnp.bfloat16),
            *scratch_of(rows),
        ],
        name="attend_own",
        **params_of(kv_heads * group, rows, 1, OWN_VMEM_LIMIT),
    )(flags, queries, keys, values)
    return [states[5 * h:5 * h + 5] for h in range(kv_heads)]


def chip_pairs(flags, keys, values, got, kv_heads, shared):
    rows = keys.shape[0]
    *pairs, span = pl.pallas_call(
        functools.partial(pair_kernel, kv_heads, shared),
        in_specs=[SMEM, VMEM, VMEM, VMEM],
        out_specs=[VMEM] * kv_heads + [SMEM],
        out_shape=[jax.ShapeDtypeStruct((2, rows, 2 * HEAD_SIZE), jnp.bfloat16)] * kv_heads
        + [jax.ShapeDtypeStruct((1,), jnp.int32)],
        compiler_params=pltpu.CompilerParams(vmem_limit_bytes=8 * MIB),
        name="chip_pairs",
    )(flags, keys, values, got)
    return pairs, span[0]


def phase(jobs, flags, received, kvs, states, placed, width, group, kv_heads):
    rows = states[0][0].shape[2]
    span = group * HEAD_SIZE
    ends, opens = jobs[0][1] == BEYOND, jobs[-1][1] == OTHER
    args, in_specs = [flags], [SMEM]
    if opens:
        args, in_specs = args + [received], in_specs + [VMEM]
    out_shape, out_specs, aliases, where = [], [], {}, []
    for (h, stage), kv in zip(jobs, kvs):
        for at in WRITTEN[stage]:
            aliases[len(args) + 1 + at] = len(out_shape)
            where.append((h, at))
            out_shape.append(state_shapes(group, rows)[at])
            out_specs.append(VMEM)
        args += [kv, *states[h]]
        in_specs += [VMEM] * 6
    scratch = scratch_of(rows)
    if ends:
        if placed is not None:
            aliases[len(args)] = len(out_shape)
            args, in_specs = args + [placed], in_specs + [HBM]
        out_shape += [
            jax.ShapeDtypeStruct((rows, width), jnp.bfloat16),
            jax.ShapeDtypeStruct((rows, span), jnp.bfloat16),
        ]
        out_specs += [HBM, HBM]
        scratch = [
            pltpu.VMEM((2, rows, span), jnp.bfloat16),
            pltpu.SemaphoreType.DMA((2,)),
            *scratch,
        ]
    results = pl.pallas_call(
        functools.partial(phase_kernel, jobs, kv_heads, int(placed is not None and ends)),
        in_specs=in_specs,
        out_specs=out_specs,
        out_shape=out_shape,
        scratch_shapes=scratch,
        input_output_aliases=aliases,
        name="attend" + "".join(f"_{'other second first beyond'.split()[k]}{h}" for h, k in jobs),
        **params_of(2 * group, rows, 1),
    )(*args)
    for (h, at), result in zip(where, results):
        states[h][at] = result
    return results[len(where):]


def cut_out(flags, queries):
    rows, width = queries.shape
    return pl.pallas_call(
        cut_kernel,
        in_specs=[SMEM, HBM],
        out_specs=VMEM,
        out_shape=jax.ShapeDtypeStruct((rows, width // 2), queries.dtype),
        scratch_shapes=[pltpu.SemaphoreType.DMA((1,))],
        compiler_params=pltpu.CompilerParams(vmem_limit_bytes=CUT_VMEM_LIMIT),
        name="cut_queries",
    )(flags, queries)


def put_in(flags, pieces, out):
    return pl.pallas_call(
        place_kernel,
        in_specs=[SMEM] + [VMEM] * len(pieces) + [HBM],
        out_specs=HBM,
        out_shape=jax.ShapeDtypeStruct(out.shape, out.dtype),
        scratch_shapes=[pltpu.SemaphoreType.DMA((len(pieces),))],
        input_output_aliases={1 + len(pieces): 0},
        compiler_params=pltpu.CompilerParams(vmem_limit_bytes=4 * MIB),
        name="place_result",
    )(flags, *pieces, out)


def on_device(queries, keys, values, prefix_spans):
    rows, width = queries.shape
    length = lax.axis_size("ctx")
    kv_local = keys.shape[1] // HEAD_SIZE
    shared = kv_local % 2 == 1
    kv_heads, group = (kv_local, GROUP // 2) if shared else (kv_local // 2, GROUP)
    q_width, kv_width = width // 2, kv_heads * HEAD_SIZE

    position = lax.axis_index("ctx")
    core = position % 2
    lower = (position // 2) % 2 == 0
    swap = [(i, i ^ 1) for i in range(length)]
    across = [(i, i ^ 2) for i in range(length)]
    ahead = [(i, i + 4) for i in range(length - 4)]

    def theirs(a):
        return a if shared else jnp.where(core == 0, a[:, kv_width:], a[:, :kv_width])

    span_columns = jnp.broadcast_to(prefix_spans.astype(jnp.bfloat16), (rows, HEAD_SIZE))
    core_flag = core[None].astype(jnp.int32)
    kv_sent = jnp.concatenate([theirs(keys), theirs(values), span_columns], axis=1)
    kv_got, cut_flag = lax.optimization_barrier((moved(kv_sent, swap), core_flag))
    q_got = moved(cut_out(cut_flag, queries), swap)
    pairs, other_span = chip_pairs(core_flag, keys, values, kv_got, kv_heads, shared)

    reach_own = jnp.minimum(prefix_spans[0], position)
    reach_other = jnp.minimum(other_span, position ^ 1)

    def counts(distance):
        first = 2 * distance - 1
        return [
            jnp.clip(reach_own - first - core + 1, 0, 2),
            jnp.clip(reach_other - first - (1 - core) + 1, 0, 2),
        ]

    flags = jnp.stack([core, *[n for d in range(1, 5) for n in counts(d)]]).astype(jnp.int32)

    def across_of(pair, second):
        return moved(jnp.where(lower, pair, second), across)

    heads = range(kv_heads)
    second = [moved(pairs[h], ahead) for h in heads]
    states = own_attention(core_flag, queries, keys, values, group, kv_heads, shared)
    states = [list(state) for state in states]
    first, beyond, out, returned = {}, {}, None, []
    for t in range(kv_heads + 3):
        jobs = [(h, t - h) for h in heads if 0 <= t - h <= BEYOND]
        arrived = [[pairs, second, first, beyond][stage][h] for h, stage in jobs]
        if t > 0:
            arrived, states = lax.optimization_barrier((arrived, states))
        for (h, stage), kv in zip(jobs, arrived):
            if stage == SECOND:
                second[h] = kv
                first[h] = across_of(pairs[h], kv)
            if stage == FIRST:
                beyond[h] = moved(jnp.concatenate([kv, second[h][:1]]), ahead)
        done = phase(jobs, flags, q_got, arrived, states, out, width, group, kv_heads)
        if done:
            out = done[0]
            returned.append(moved(done[1], swap))
    return put_in(core_flag, returned, out)


def solution(mesh):
    placed = (P("ctx", "tp"), P("ctx", "tp"), P("ctx", "tp"), P("ctx"))
    return jax.shard_map(
        on_device, mesh=mesh, in_specs=placed, out_specs=P("ctx", "tp"), check_vma=False
    )
```

```python
import functools
import math

import jax
import jax.numpy as jnp
from jax import lax
from jax.experimental import pallas as pl
from jax.experimental.pallas import tpu as pltpu
from jax.sharding import PartitionSpec as P

QUERY_HEAD_COUNT = 64
KEY_VALUE_HEADS = 8
HEAD_SIZE = 128
GROUP = QUERY_HEAD_COUNT // KEY_VALUE_HEADS
SCALE = math.log2(math.e) / math.sqrt(HEAD_SIZE)
EXPONENT_ROOM = 100.0
ONES_ROWS = 16
MIB = 1024 * 1024
VMEM_LIMIT = 10 * MIB
CUT_VMEM_LIMIT = 60 * MIB
OWN_VMEM_LIMIT = 30 * MIB


def moved(shard, pairs):
    return lax.ppermute(shard, "ctx", pairs)


def head_rows(i):
    return slice(i * HEAD_SIZE, (i + 1) * HEAD_SIZE)


def column_max(s):
    return jnp.max(s, axis=0, keepdims=True)


def column_sum(s):
    return jnp.sum(s, axis=0, keepdims=True)


def dot(a, b):
    return jnp.dot(a, b, preferred_element_type=jnp.float32)


class Step:
    def __init__(self, refs, kv_ref, slot, head, at):
        self.qt_ref, self.acc_ref, self.m_ref, self.l_ref, s_refs, vt_refs = refs
        self.kv_ref, self.slot, self.head = kv_ref, slot, head
        self.s_ref, self.vt_ref = s_refs[at % 2], vt_refs[slot % 2]
        self.rows = self.qt_ref.shape[1]
        self.half = self.rows // 2

    def keys(self, c):
        return self.kv_ref[self.slot, c * self.half:(c + 1) * self.half, :HEAD_SIZE]

    def chunk(self, c):
        return slice(c * self.half, (c + 1) * self.half)

    @property
    def row(self):
        return slice(self.head, self.head + 1)


class DiagonalStep(Step):
    def scores(self, c):
        half = self.half
        lower = lax.broadcasted_iota(jnp.int32, (half, half), 0) <= lax.broadcasted_iota(
            jnp.int32, (half, half), 1
        )
        qt = self.qt_ref[head_rows(self.head), :]
        if c == 0:
            near = jnp.where(lower, dot(self.keys(0), qt[:, :half]), -jnp.inf)
            over = dot(self.keys(0), qt[:, half:])
            self.s_ref[:half, :half] = near
            self.s_ref[:half, half:] = over
            return jnp.concatenate([column_max(near), column_max(over)], axis=1)
        far = jnp.where(lower, dot(self.keys(1), qt[:, half:]), -jnp.inf)
        self.s_ref[half:, half:] = far
        return jnp.concatenate([jnp.full((1, half), -jnp.inf, jnp.float32), column_max(far)], axis=1)

    def start(self, top):
        self.m = top * SCALE

    def weigh(self, c):
        half = self.half
        if c == 0:
            p = jnp.exp2(self.s_ref[:half, :] * SCALE - self.m)
            self.l0 = column_sum(p)
            self.p0 = p.astype(jnp.bfloat16)
        else:
            p = jnp.exp2(self.s_ref[half:, half:] * SCALE - self.m[:, half:])
            self.l1 = column_sum(p)
            self.p1 = p.astype(jnp.bfloat16)

    def finish(self):
        half = self.half
        at = head_rows(self.head)
        self.acc_ref[at, :half] = dot(self.vt_ref[:HEAD_SIZE, :half], self.p0[:, :half])
        self.acc_ref[at, half:] = dot(
            self.vt_ref[:HEAD_SIZE, :], jnp.concatenate([self.p0[:, half:], self.p1], axis=0)
        )
        self.m_ref[self.row, :] = self.m
        self.l_ref[self.row, :half] = self.l0[:, :half]
        self.l_ref[self.row, half:] = self.l0[:, half:] + self.l1


def run_diagonal(refs, kv_ref, slot):
    refs[5][slot % 2][:HEAD_SIZE, :] = kv_ref[slot, :, HEAD_SIZE:].T
    steps = [DiagonalStep(refs, kv_ref, slot, i, i) for i in range(refs[2].shape[0])]
    top = jnp.maximum(steps[0].scores(0), steps[0].scores(1))
    for now, after in zip(steps, steps[1:] + [None]):
        now.start(top)
        tops = []
        for c in range(2):
            if after is not None:
                tops.append(after.scores(c))
            now.weigh(c)
        now.finish()
        if tops:
            top = jnp.maximum(*tops)


def run_bounded(refs, kv_ref, slots):
    qt_ref, acc_ref, m_ref, l_ref, _, vt_refs = refs
    heads, rows = m_ref.shape
    half = rows // 2

    def weights(slot, i):
        qt = qt_ref[head_rows(i), :]
        m = m_ref[i:i + 1, :]
        parts = []
        for c in range(2):
            s = dot(kv_ref[slot, c * half:(c + 1) * half, :HEAD_SIZE], qt)
            parts.append(jnp.exp2(s * SCALE - m).astype(jnp.bfloat16))
        return jnp.concatenate(parts, axis=0)

    def add(slot, i, w):
        o = dot(vt_refs[slot % 2][...], w)
        acc_ref[head_rows(i), :] += o[:HEAD_SIZE, :]
        l_ref[i:i + 1, :] += o[HEAD_SIZE:HEAD_SIZE + 1, :]

    waiting = None
    for slot in slots:
        vt_refs[slot % 2][:HEAD_SIZE, :] = kv_ref[slot, :, HEAD_SIZE:].T
        for i in range(heads):
            w = weights(slot, i)
            if waiting is not None:
                add(*waiting)
            waiting = (slot, i, w)
    add(*waiting)


def run_exact(refs, kv_ref, slots):
    qt_ref, acc_ref, m_ref, l_ref, _, vt_refs = refs
    for slot in slots:
        vt_refs[slot % 2][:HEAD_SIZE, :] = kv_ref[slot, :, HEAD_SIZE:].T

        def head(i, carry, slot=slot):
            at = pl.ds(pl.multiple_of(i * HEAD_SIZE, HEAD_SIZE), HEAD_SIZE)
            row = pl.ds(i, 1)
            s = dot(kv_ref[slot, :, :HEAD_SIZE], qt_ref[at, :]) * SCALE
            m_old = m_ref[row, :]
            m = jnp.maximum(m_old, column_max(s))
            correct = jnp.exp2(m_old - m)
            o = dot(vt_refs[slot % 2][...], jnp.exp2(s - m).astype(jnp.bfloat16))
            acc_ref[at, :] = acc_ref[at, :] * correct + o[:HEAD_SIZE, :]
            l_ref[row, :] = l_ref[row, :] * correct + o[HEAD_SIZE:HEAD_SIZE + 1, :]
            m_ref[row, :] = m
            return carry

        lax.fori_loop(0, m_ref.shape[0], head, 0)


def run_whole(refs, bound_ref, kv_ref, slots):
    longest = 0.0
    for slot in slots:
        k = kv_ref[slot, :, :HEAD_SIZE].astype(jnp.float32)
        longest = jnp.maximum(longest, jnp.max(jnp.sum(k * k, axis=1, keepdims=True)))
    longest = jnp.sqrt(jnp.full((1, 1), longest, jnp.float32))
    bounded = jnp.max(bound_ref[...] * longest - refs[2][...]) <= EXPONENT_ROOM
    pl.when(bounded)(lambda: run_bounded(refs, kv_ref, slots))
    pl.when(jnp.logical_not(bounded))(lambda: run_exact(refs, kv_ref, slots))


def fill_ones(vt_refs):
    for vt_ref in vt_refs:
        vt_ref[HEAD_SIZE:, :] = jnp.ones((ONES_ROWS, vt_ref.shape[1]), jnp.bfloat16)


def refs_for(work, b):
    qt_ref, acc_ref, m_ref, l_ref, *rest = work
    return (qt_ref.at[b], acc_ref.at[b], m_ref.at[b], l_ref.at[b], rest[:2], rest[2:])


def turn(q_ref, qt_ref, bound_ref):
    for i in range(q_ref.shape[1] // HEAD_SIZE):
        qt = q_ref[:, head_rows(i)].T
        qt_ref[head_rows(i), :] = qt
        wide = qt.astype(jnp.float32)
        bound_ref[i:i + 1, :] = jnp.sqrt(column_sum(wide * wide)) * (SCALE * 1.01)


def own_kernel(kv_heads, shared, flags, queries, keys, values, *refs):
    states, (q_buf, arrived, kv_buf, *scratch) = refs[:5 * kv_heads], refs[5 * kv_heads:]
    core = flags[0]
    span = q_buf.shape[2]
    copies = []
    for h in range(kv_heads):
        at = pl.multiple_of((core * kv_heads + h) * span, span)
        head = h if shared else core * kv_heads + h
        kv_at = pl.ds(pl.multiple_of(head * HEAD_SIZE, HEAD_SIZE), HEAD_SIZE)
        moves = [
            (queries.at[:, pl.ds(at, span)], q_buf.at[h]),
            (keys.at[:, kv_at], kv_buf.at[h, :, :HEAD_SIZE]),
            (values.at[:, kv_at], kv_buf.at[h, :, HEAD_SIZE:]),
        ]
        copies.append(
            [pltpu.make_async_copy(*move, arrived.at[3 * h + i]) for i, move in enumerate(moves)]
        )
        for copy in copies[h]:
            copy.start()
    for h in range(kv_heads):
        qt_ref, bound_ref, acc_ref, m_ref, l_ref = [ref.at[0] for ref in states[5 * h:5 * h + 5]]
        for copy in copies[h]:
            copy.wait()
        turn(q_buf.at[h], qt_ref, bound_ref)
        run_diagonal((qt_ref, acc_ref, m_ref, l_ref, scratch[:2], scratch[2:]), kv_buf, h)


def pair_kernel(kv_heads, shared, flags, keys, values, got, *refs):
    *pairs, span = refs
    core = flags[0]
    for h, pair in enumerate(pairs):
        at = head_rows(h)
        head = h if shared else core * kv_heads + h
        kv_at = pl.ds(pl.multiple_of(head * HEAD_SIZE, HEAD_SIZE), HEAD_SIZE)
        mine = 1 - core
        pair[mine, :, :HEAD_SIZE] = keys[:, kv_at]
        pair[mine, :, HEAD_SIZE:] = values[:, kv_at]
        pair[core, :, :HEAD_SIZE] = got[:, at]
        pair[core, :, HEAD_SIZE:] = got[:, head_rows(kv_heads + h)]
    last = got[:16, head_rows(2 * kv_heads)].astype(jnp.float32)
    span[0] = jnp.max(last).astype(jnp.int32)


def add_other(h, flags, received, kv_ref, bound_ref, work):
    core = flags[0]
    span = work[0].shape[1]
    turn(received.at[:, h * span:(h + 1) * span], work[0].at[1], bound_ref.at[1])
    pl.when(core == 0)(lambda: run_diagonal(refs_for(work, 1), kv_ref, 0))
    pl.when(core == 1)(lambda: run_diagonal(refs_for(work, 1), kv_ref, 1))
    odd = 1 - core
    run_whole(refs_for(work, odd), bound_ref.at[odd], kv_ref, [1])


def add_window(flags, work, bound_ref, kv_ref, pieces, b):
    refs = refs_for(work, b)
    for distance, slots in pieces:
        count = flags[2 * distance - 1 + b]
        for most in range(1, len(slots) + 1):
            add = functools.partial(run_whole, refs, bound_ref.at[b], kv_ref, slots[:most])
            pl.when(count == most)(add)
    return refs


OTHER, SECOND, FIRST, BEYOND = range(4)
PIECES = {SECOND: [(2, [0, 1])], FIRST: [(1, [0, 1])], BEYOND: [(3, [0, 1]), (4, [2])]}
WRITTEN = {OTHER: range(5), SECOND: range(2, 5), FIRST: range(2, 5), BEYOND: ()}


def phase_kernel(jobs, kv_heads, placed, flags, *refs):
    refs = list(refs)
    take = lambda n: [refs.pop(0) for _ in range(n)]
    received = take(1)[0] if jobs[-1][1] == OTHER else None
    inputs = [take(6) for _ in jobs]
    take(placed)
    outputs = [take(len(WRITTEN[stage])) for _, stage in jobs]
    if jobs[0][1] == BEYOND:
        out, other, stage_buf, sent = take(4)
    scratch = refs
    fill_ones(scratch[2:])
    for (h, stage), (kv_ref, *state), new in zip(jobs, inputs, outputs):
        for at, ref in zip(WRITTEN[stage], new):
            state[at] = ref
        qt_ref, bound_ref, acc_ref, m_ref, l_ref = state
        work = (qt_ref, acc_ref, m_ref, l_ref, *scratch)
        if stage == OTHER:
            add_other(h, flags, received, kv_ref, bound_ref, work)
            continue

        def block(b, carry, stage=stage, work=work, bound_ref=bound_ref, kv_ref=kv_ref):
            _, acc_ref, _, l_ref, *_ = add_window(flags, work, bound_ref, kv_ref, PIECES[stage], b)
            if stage == BEYOND:
                for i in range(stage_buf.shape[2] // HEAD_SIZE):
                    result = acc_ref[head_rows(i), :] / l_ref[i:i + 1, :]
                    stage_buf[b, :, head_rows(i)] = result.T.astype(stage_buf.dtype)
            return carry

        lax.fori_loop(0, 2, block, 0)
        if stage == BEYOND:
            span = stage_buf.shape[2]
            own_at = pl.multiple_of((flags[0] * kv_heads + h) * span, span)
            copies = [
                pltpu.make_async_copy(stage_buf.at[0], out.at[:, pl.ds(own_at, span)], sent.at[0]),
                pltpu.make_async_copy(stage_buf.at[1], other, sent.at[1]),
            ]
            for copy in copies:
                copy.start()
    if jobs[0][1] == BEYOND:
        for copy in copies:
            copy.wait()


def cut_kernel(flags, queries, out, done):
    width = out.shape[1]
    at = pl.multiple_of((1 - flags[0]) * width, width)
    copy = pltpu.make_async_copy(queries.at[:, pl.ds(at, width)], out, done.at[0])
    copy.start()
    copy.wait()


def place_kernel(flags, *refs):
    *pieces, _, out, done = refs
    width = pieces[0].shape[1]
    copies = []
    for i, piece in enumerate(pieces):
        at = pl.multiple_of(((1 - flags[0]) * len(pieces) + i) * width, width)
        copies.append(pltpu.make_async_copy(piece, out.at[:, pl.ds(at, width)], done.at[i]))
    for copy in copies:
        copy.start()
    for copy in copies:
        copy.wait()


SMEM = pl.BlockSpec(memory_space=pltpu.SMEM)
VMEM = pl.BlockSpec(memory_space=pltpu.VMEM)
HBM = pl.BlockSpec(memory_space=pltpu.HBM)


def scratch_of(rows):
    return [
        pltpu.VMEM((rows, rows), jnp.float32),
        pltpu.VMEM((rows, rows), jnp.float32),
        pltpu.VMEM((HEAD_SIZE + ONES_ROWS, rows), jnp.bfloat16),
        pltpu.VMEM((HEAD_SIZE + ONES_ROWS, rows), jnp.bfloat16),
    ]


def params_of(heads, rows, blocks, limit=VMEM_LIMIT):
    return dict(
        compiler_params=pltpu.CompilerParams(vmem_limit_bytes=limit),
        cost_estimate=pl.CostEstimate(
            flops=int(heads * rows * HEAD_SIZE * blocks),
            bytes_accessed=heads * rows,
            transcendentals=0,
        ),
    )


def state_shapes(group, rows):
    span = group * HEAD_SIZE
    stats = jax.ShapeDtypeStruct((2, group, rows), jnp.float32)
    return [
        jax.ShapeDtypeStruct((2, span, rows), jnp.bfloat16),
        stats,
        jax.ShapeDtypeStruct((2, span, rows), jnp.float32),
        stats,
        stats,
    ]


def own_attention(flags, queries, keys, values, group, kv_heads, shared):
    rows = queries.shape[0]
    span = group * HEAD_SIZE
    states = pl.pallas_call(
        functools.partial(own_kernel, kv_heads, shared),
        in_specs=[SMEM, HBM, HBM, HBM],
        out_specs=[VMEM] * (5 * kv_heads),
        out_shape=state_shapes(group, rows) * kv_heads,
        scratch_shapes=[
            pltpu.VMEM((kv_heads, rows, span), jnp.bfloat16),
            pltpu.SemaphoreType.DMA((3 * kv_heads,)),
            pltpu.VMEM((kv_heads, rows, 2 * HEAD_SIZE), jnp.bfloat16),
            *scratch_of(rows),
        ],
        name="attend_own",
        **params_of(kv_heads * group, rows, 1, OWN_VMEM_LIMIT),
    )(flags, queries, keys, values)
    return [states[5 * h:5 * h + 5] for h in range(kv_heads)]


def chip_pairs(flags, keys, values, got, kv_heads, shared):
    rows = keys.shape[0]
    *pairs, span = pl.pallas_call(
        functools.partial(pair_kernel, kv_heads, shared),
        in_specs=[SMEM, VMEM, VMEM, VMEM],
        out_specs=[VMEM] * kv_heads + [SMEM],
        out_shape=[jax.ShapeDtypeStruct((2, rows, 2 * HEAD_SIZE), jnp.bfloat16)] * kv_heads
        + [jax.ShapeDtypeStruct((1,), jnp.int32)],
        compiler_params=pltpu.CompilerParams(vmem_limit_bytes=8 * MIB),
        name="chip_pairs",
    )(flags, keys, values, got)
    return pairs, span[0]


def phase(jobs, flags, received, kvs, states, placed, width, group, kv_heads):
    rows = states[0][0].shape[2]
    span = group * HEAD_SIZE
    ends, opens = jobs[0][1] == BEYOND, jobs[-1][1] == OTHER
    args, in_specs = [flags], [SMEM]
    if opens:
        args, in_specs = args + [received], in_specs + [VMEM]
    out_shape, out_specs, aliases, where = [], [], {}, []
    for (h, stage), kv in zip(jobs, kvs):
        for at in WRITTEN[stage]:
            aliases[len(args) + 1 + at] = len(out_shape)
            where.append((h, at))
            out_shape.append(state_shapes(group, rows)[at])
            out_specs.append(VMEM)
        args += [kv, *states[h]]
        in_specs += [VMEM] * 6
    scratch = scratch_of(rows)
    if ends:
        if placed is not None:
            aliases[len(args)] = len(out_shape)
            args, in_specs = args + [placed], in_specs + [HBM]
        out_shape += [
            jax.ShapeDtypeStruct((rows, width), jnp.bfloat16),
            jax.ShapeDtypeStruct((rows, span), jnp.bfloat16),
        ]
        out_specs += [HBM, HBM]
        scratch = [
            pltpu.VMEM((2, rows, span), jnp.bfloat16),
            pltpu.SemaphoreType.DMA((2,)),
            *scratch,
        ]
    results = pl.pallas_call(
        functools.partial(phase_kernel, jobs, kv_heads, int(placed is not None and ends)),
        in_specs=in_specs,
        out_specs=out_specs,
        out_shape=out_shape,
        scratch_shapes=scratch,
        input_output_aliases=aliases,
        name="attend" + "".join(f"_{'other second first beyond'.split()[k]}{h}" for h, k in jobs),
        **params_of(2 * group, rows, 1),
    )(*args)
    for (h, at), result in zip(where, results):
        states[h][at] = result
    return results[len(where):]


def cut_out(flags, queries):
    rows, width = queries.shape
    return pl.pallas_call(
        cut_kernel,
        in_specs=[SMEM, HBM],
        out_specs=VMEM,
        out_shape=jax.ShapeDtypeStruct((rows, width // 2), queries.dtype),
        scratch_shapes=[pltpu.SemaphoreType.DMA((1,))],
        compiler_params=pltpu.CompilerParams(vmem_limit_bytes=CUT_VMEM_LIMIT),
        name="cut_queries",
    )(flags, queries)


def put_in(flags, pieces, out):
    return pl.pallas_call(
        place_kernel,
        in_specs=[SMEM] + [VMEM] * len(pieces) + [HBM],
        out_specs=HBM,
        out_shape=jax.ShapeDtypeStruct(out.shape, out.dtype),
        scratch_shapes=[pltpu.SemaphoreType.DMA((len(pieces),))],
        input_output_aliases={1 + len(pieces): 0},
        compiler_params=pltpu.CompilerParams(vmem_limit_bytes=4 * MIB),
        name="place_result",
    )(flags, *pieces, out)


def on_device(queries, keys, values, prefix_spans):
    rows, width = queries.shape
    length = lax.axis_size("ctx")
    kv_local = keys.shape[1] // HEAD_SIZE
    shared = kv_local % 2 == 1
    kv_heads, group = (kv_local, GROUP // 2) if shared else (kv_local // 2, GROUP)
    q_width, kv_width = width // 2, kv_heads * HEAD_SIZE

    position = lax.axis_index("ctx")
    core = position % 2
    lower = (position // 2) % 2 == 0
    swap = [(i, i ^ 1) for i in range(length)]
    across = [(i, i ^ 2) for i in range(length)]
    ahead = [(i, i + 4) for i in range(length - 4)]

    def theirs(a):
        return a if shared else jnp.where(core == 0, a[:, kv_width:], a[:, :kv_width])

    span_columns = jnp.broadcast_to(prefix_spans.astype(jnp.bfloat16), (rows, HEAD_SIZE))
    core_flag = core[None].astype(jnp.int32)
    kv_sent = jnp.concatenate([theirs(keys), theirs(values), span_columns], axis=1)
    kv_got, cut_flag = lax.optimization_barrier((moved(kv_sent, swap), core_flag))
    q_got = moved(cut_out(cut_flag, queries), swap)
    pairs, other_span = chip_pairs(core_flag, keys, values, kv_got, kv_heads, shared)

    reach_own = jnp.minimum(prefix_spans[0], position)
    reach_other = jnp.minimum(other_span, position ^ 1)

    def counts(distance):
        first = 2 * distance - 1
        return [
            jnp.clip(reach_own - first - core + 1, 0, 2),
            jnp.clip(reach_other - first - (1 - core) + 1, 0, 2),
        ]

    flags = jnp.stack([core, *[n for d in range(1, 5) for n in counts(d)]]).astype(jnp.int32)

    def across_of(pair, second):
        return moved(jnp.where(lower, pair, second), across)

    heads = range(kv_heads)
    second = [moved(pairs[h], ahead) for h in heads]
    states = own_attention(core_flag, queries, keys, values, group, kv_heads, shared)
    states = [list(state) for state in states]
    first, beyond, out, returned = {}, {}, None, []
    for t in range(kv_heads + 3):
        jobs = [(h, t - h) for h in heads if 0 <= t - h <= BEYOND]
        arrived = [[pairs, second, first, beyond][stage][h] for h, stage in jobs]
        if t > 0:
            arrived, states = lax.optimization_barrier((arrived, states))
        for (h, stage), kv in zip(jobs, arrived):
            if stage == SECOND:
                second[h] = kv
                first[h] = across_of(pairs[h], kv)
            if stage == FIRST:
                beyond[h] = moved(jnp.concatenate([kv, second[h][:1]]), ahead)
        done = phase(jobs, flags, q_got, arrived, states, out, width, group, kv_heads)
        if done:
            out = done[0]
            returned.append(moved(done[1], swap))
    return put_in(core_flag, returned, out)


def solution(mesh):
    placed = (P("ctx", "tp"), P("ctx", "tp"), P("ctx", "tp"), P("ctx"))
    return jax.shard_map(
        on_device, mesh=mesh, in_specs=placed, out_specs=P("ctx", "tp"), check_vma=False
    )
```

```python
import functools
import math

import jax
import jax.numpy as jnp
from jax import lax
from jax.experimental import pallas as pl
from jax.experimental.pallas import tpu as pltpu
from jax.sharding import PartitionSpec as P

QUERY_HEAD_COUNT = 64
KEY_VALUE_HEADS = 8
HEAD_SIZE = 128
GROUP = QUERY_HEAD_COUNT // KEY_VALUE_HEADS
SCALE = math.log2(math.e) / math.sqrt(HEAD_SIZE)
EXPONENT_ROOM = 100.0
ONES_ROWS = 16
MIB = 1024 * 1024
VMEM_LIMIT = 10 * MIB
CUT_VMEM_LIMIT = 60 * MIB
OWN_VMEM_LIMIT = 10 * MIB


def moved(shard, pairs):
    return lax.ppermute(shard, "ctx", pairs)


def head_rows(i):
    return slice(i * HEAD_SIZE, (i + 1) * HEAD_SIZE)


def column_max(s):
    return jnp.max(s, axis=0, keepdims=True)


def column_sum(s):
    return jnp.sum(s, axis=0, keepdims=True)


def dot(a, b):
    return jnp.dot(a, b, preferred_element_type=jnp.float32)


class Step:
    def __init__(self, refs, kv_ref, slot, head, at):
        self.qt_ref, self.acc_ref, self.m_ref, self.l_ref, s_refs, vt_refs = refs
        self.kv_ref, self.slot, self.head = kv_ref, slot, head
        self.s_ref, self.vt_ref = s_refs[at % 2], vt_refs[slot % 2]
        self.rows = self.qt_ref.shape[1]
        self.half = self.rows // 2

    def keys(self, c):
        return self.kv_ref[self.slot, c * self.half:(c + 1) * self.half, :HEAD_SIZE]

    def chunk(self, c):
        return slice(c * self.half, (c + 1) * self.half)

    @property
    def row(self):
        return slice(self.head, self.head + 1)


class DiagonalStep(Step):
    def scores(self, c):
        half = self.half
        lower = lax.broadcasted_iota(jnp.int32, (half, half), 0) <= lax.broadcasted_iota(
            jnp.int32, (half, half), 1
        )
        qt = self.qt_ref[head_rows(self.head), :]
        if c == 0:
            near = jnp.where(lower, dot(self.keys(0), qt[:, :half]), -jnp.inf)
            over = dot(self.keys(0), qt[:, half:])
            self.s_ref[:half, :half] = near
            self.s_ref[:half, half:] = over
            return jnp.concatenate([column_max(near), column_max(over)], axis=1)
        far = jnp.where(lower, dot(self.keys(1), qt[:, half:]), -jnp.inf)
        self.s_ref[half:, half:] = far
        return jnp.concatenate([jnp.full((1, half), -jnp.inf, jnp.float32), column_max(far)], axis=1)

    def start(self, top):
        self.m = top * SCALE

    def weigh(self, c):
        half = self.half
        if c == 0:
            p = jnp.exp2(self.s_ref[:half, :] * SCALE - self.m)
            self.l0 = column_sum(p)
            self.p0 = p.astype(jnp.bfloat16)
        else:
            p = jnp.exp2(self.s_ref[half:, half:] * SCALE - self.m[:, half:])
            self.l1 = column_sum(p)
            self.p1 = p.astype(jnp.bfloat16)

    def finish(self):
        half = self.half
        at = head_rows(self.head)
        self.acc_ref[at, :half] = dot(self.vt_ref[:HEAD_SIZE, :half], self.p0[:, :half])
        self.acc_ref[at, half:] = dot(
            self.vt_ref[:HEAD_SIZE, :], jnp.concatenate([self.p0[:, half:], self.p1], axis=0)
        )
        self.m_ref[self.row, :] = self.m
        self.l_ref[self.row, :half] = self.l0[:, :half]
        self.l_ref[self.row, half:] = self.l0[:, half:] + self.l1


def run_diagonal(refs, kv_ref, slot):
    refs[5][slot % 2][:HEAD_SIZE, :] = kv_ref[slot, :, HEAD_SIZE:].T
    steps = [DiagonalStep(refs, kv_ref, slot, i, i) for i in range(refs[2].shape[0])]
    top = jnp.maximum(steps[0].scores(0), steps[0].scores(1))
    for now, after in zip(steps, steps[1:] + [None]):
        now.start(top)
        tops = []
        for c in range(2):
            if after is not None:
                tops.append(after.scores(c))
            now.weigh(c)
        now.finish()
        if tops:
            top = jnp.maximum(*tops)


def run_bounded(refs, kv_ref, slots):
    qt_ref, acc_ref, m_ref, l_ref, _, vt_refs = refs
    heads, rows = m_ref.shape
    half = rows // 2

    def weights(slot, i):
        qt = qt_ref[head_rows(i), :]
        m = m_ref[i:i + 1, :]
        parts = []
        for c in range(2):
            s = dot(kv_ref[slot, c * half:(c + 1) * half, :HEAD_SIZE], qt)
            parts.append(jnp.exp2(s * SCALE - m).astype(jnp.bfloat16))
        return jnp.concatenate(parts, axis=0)

    def add(slot, i, w):
        o = dot(vt_refs[slot % 2][...], w)
        acc_ref[head_rows(i), :] += o[:HEAD_SIZE, :]
        l_ref[i:i + 1, :] += o[HEAD_SIZE:HEAD_SIZE + 1, :]

    waiting = None
    for slot in slots:
        vt_refs[slot % 2][:HEAD_SIZE, :] = kv_ref[slot, :, HEAD_SIZE:].T
        for i in range(heads):
            w = weights(slot, i)
            if waiting is not None:
                add(*waiting)
            waiting = (slot, i, w)
    add(*waiting)


def run_exact(refs, kv_ref, slots):
    qt_ref, acc_ref, m_ref, l_ref, _, vt_refs = refs
    for slot in slots:
        vt_refs[slot % 2][:HEAD_SIZE, :] = kv_ref[slot, :, HEAD_SIZE:].T

        def head(i, carry, slot=slot):
            at = pl.ds(pl.multiple_of(i * HEAD_SIZE, HEAD_SIZE), HEAD_SIZE)
            row = pl.ds(i, 1)
            s = dot(kv_ref[slot, :, :HEAD_SIZE], qt_ref[at, :]) * SCALE
            m_old = m_ref[row, :]
            m = jnp.maximum(m_old, column_max(s))
            correct = jnp.exp2(m_old - m)
            o = dot(vt_refs[slot % 2][...], jnp.exp2(s - m).astype(jnp.bfloat16))
            acc_ref[at, :] = acc_ref[at, :] * correct + o[:HEAD_SIZE, :]
            l_ref[row, :] = l_ref[row, :] * correct + o[HEAD_SIZE:HEAD_SIZE + 1, :]
            m_ref[row, :] = m
            return carry

        lax.fori_loop(0, m_ref.shape[0], head, 0)


def run_whole(refs, bound_ref, kv_ref, slots):
    longest = 0.0
    for slot in slots:
        k = kv_ref[slot, :, :HEAD_SIZE].astype(jnp.float32)
        longest = jnp.maximum(longest, jnp.max(jnp.sum(k * k, axis=1, keepdims=True)))
    longest = jnp.sqrt(jnp.full((1, 1), longest, jnp.float32))
    bounded = jnp.max(bound_ref[...] * longest - refs[2][...]) <= EXPONENT_ROOM
    pl.when(bounded)(lambda: run_bounded(refs, kv_ref, slots))
    pl.when(jnp.logical_not(bounded))(lambda: run_exact(refs, kv_ref, slots))


def fill_ones(vt_refs):
    for vt_ref in vt_refs:
        vt_ref[HEAD_SIZE:, :] = jnp.ones((ONES_ROWS, vt_ref.shape[1]), jnp.bfloat16)


def refs_for(work, b):
    qt_ref, acc_ref, m_ref, l_ref, *rest = work
    return (qt_ref.at[b], acc_ref.at[b], m_ref.at[b], l_ref.at[b], rest[:2], rest[2:])


def turn(q_ref, qt_ref, bound_ref):
    for i in range(q_ref.shape[1] // HEAD_SIZE):
        qt = q_ref[:, head_rows(i)].T
        qt_ref[head_rows(i), :] = qt
        wide = qt.astype(jnp.float32)
        bound_ref[i:i + 1, :] = jnp.sqrt(column_sum(wide * wide)) * (SCALE * 1.01)


def own_kernel(kv_heads, shared, flags, queries, keys, values, *refs):
    states, (q_buf, arrived, kv_buf, *scratch) = refs[:5 * kv_heads], refs[5 * kv_heads:]
    core = flags[0]
    span = q_buf.shape[2]
    copies = []
    for h in range(kv_heads):
        at = pl.multiple_of((core * kv_heads + h) * span, span)
        head = h if shared else core * kv_heads + h
        kv_at = pl.ds(pl.multiple_of(head * HEAD_SIZE, HEAD_SIZE), HEAD_SIZE)
        moves = [
            (queries.at[:, pl.ds(at, span)], q_buf.at[h]),
            (keys.at[:, kv_at], kv_buf.at[h, :, :HEAD_SIZE]),
            (values.at[:, kv_at], kv_buf.at[h, :, HEAD_SIZE:]),
        ]
        copies.append(
            [pltpu.make_async_copy(*move, arrived.at[3 * h + i]) for i, move in enumerate(moves)]
        )
        for copy in copies[h]:
            copy.start()
    for h in range(kv_heads):
        qt_ref, bound_ref, acc_ref, m_ref, l_ref = [ref.at[0] for ref in states[5 * h:5 * h + 5]]
        for copy in copies[h]:
            copy.wait()
        turn(q_buf.at[h], qt_ref, bound_ref)
        run_diagonal((qt_ref, acc_ref, m_ref, l_ref, scratch[:2], scratch[2:]), kv_buf, h)


def pair_kernel(kv_heads, shared, flags, keys, values, got, *refs):
    *pairs, span = refs
    core = flags[0]
    for h, pair in enumerate(pairs):
        at = head_rows(h)
        head = h if shared else core * kv_heads + h
        kv_at = pl.ds(pl.multiple_of(head * HEAD_SIZE, HEAD_SIZE), HEAD_SIZE)
        mine = 1 - core
        pair[mine, :, :HEAD_SIZE] = keys[:, kv_at]
        pair[mine, :, HEAD_SIZE:] = values[:, kv_at]
        pair[core, :, :HEAD_SIZE] = got[:, at]
        pair[core, :, HEAD_SIZE:] = got[:, head_rows(kv_heads + h)]
    last = got[:16, head_rows(2 * kv_heads)].astype(jnp.float32)
    span[0] = jnp.max(last).astype(jnp.int32)


def add_other(h, flags, received, kv_ref, bound_ref, work):
    core = flags[0]
    span = work[0].shape[1]
    turn(received.at[:, h * span:(h + 1) * span], work[0].at[1], bound_ref.at[1])
    pl.when(core == 0)(lambda: run_diagonal(refs_for(work, 1), kv_ref, 0))
    pl.when(core == 1)(lambda: run_diagonal(refs_for(work, 1), kv_ref, 1))
    odd = 1 - core
    run_whole(refs_for(work, odd), bound_ref.at[odd], kv_ref, [1])


def add_window(flags, work, bound_ref, kv_ref, pieces, b):
    refs = refs_for(work, b)
    for distance, slots in pieces:
        count = flags[2 * distance - 1 + b]
        for most in range(1, len(slots) + 1):
            add = functools.partial(run_whole, refs, bound_ref.at[b], kv_ref, slots[:most])
            pl.when(count == most)(add)
    return refs


OTHER, SECOND, FIRST, BEYOND = range(4)
PIECES = {SECOND: [(2, [0, 1])], FIRST: [(1, [0, 1])], BEYOND: [(3, [0, 1]), (4, [2])]}
WRITTEN = {OTHER: range(5), SECOND: range(2, 5), FIRST: range(2, 5), BEYOND: ()}


def phase_kernel(jobs, kv_heads, placed, flags, *refs):
    refs = list(refs)
    take = lambda n: [refs.pop(0) for _ in range(n)]
    received = take(1)[0] if jobs[-1][1] == OTHER else None
    inputs = [take(6) for _ in jobs]
    take(placed)
    outputs = [take(len(WRITTEN[stage])) for _, stage in jobs]
    if jobs[0][1] == BEYOND:
        out, other, stage_buf, sent = take(4)
    scratch = refs
    fill_ones(scratch[2:])
    for (h, stage), (kv_ref, *state), new in zip(jobs, inputs, outputs):
        for at, ref in zip(WRITTEN[stage], new):
            state[at] = ref
        qt_ref, bound_ref, acc_ref, m_ref, l_ref = state
        work = (qt_ref, acc_ref, m_ref, l_ref, *scratch)
        if stage == OTHER:
            add_other(h, flags, received, kv_ref, bound_ref, work)
            continue

        def block(b, carry, stage=stage, work=work, bound_ref=bound_ref, kv_ref=kv_ref):
            _, acc_ref, _, l_ref, *_ = add_window(flags, work, bound_ref, kv_ref, PIECES[stage], b)
            if stage == BEYOND:
                for i in range(stage_buf.shape[2] // HEAD_SIZE):
                    result = acc_ref[head_rows(i), :] / l_ref[i:i + 1, :]
                    stage_buf[b, :, head_rows(i)] = result.T.astype(stage_buf.dtype)
            return carry

        lax.fori_loop(0, 2, block, 0)
        if stage == BEYOND:
            span = stage_buf.shape[2]
            own_at = pl.multiple_of((flags[0] * kv_heads + h) * span, span)
            copies = [
                pltpu.make_async_copy(stage_buf.at[0], out.at[:, pl.ds(own_at, span)], sent.at[0]),
                pltpu.make_async_copy(stage_buf.at[1], other, sent.at[1]),
            ]
            for copy in copies:
                copy.start()
    if jobs[0][1] == BEYOND:
        for copy in copies:
            copy.wait()


def cut_kernel(flags, queries, out, done):
    width = out.shape[1]
    at = pl.multiple_of((1 - flags[0]) * width, width)
    copy = pltpu.make_async_copy(queries.at[:, pl.ds(at, width)], out, done.at[0])
    copy.start()
    copy.wait()


def place_kernel(flags, *refs):
    *pieces, _, out, done = refs
    width = pieces[0].shape[1]
    copies = []
    for i, piece in enumerate(pieces):
        at = pl.multiple_of(((1 - flags[0]) * len(pieces) + i) * width, width)
        copies.append(pltpu.make_async_copy(piece, out.at[:, pl.ds(at, width)], done.at[i]))
    for copy in copies:
        copy.start()
    for copy in copies:
        copy.wait()


SMEM = pl.BlockSpec(memory_space=pltpu.SMEM)
VMEM = pl.BlockSpec(memory_space=pltpu.VMEM)
HBM = pl.BlockSpec(memory_space=pltpu.HBM)


def scratch_of(rows):
    return [
        pltpu.VMEM((rows, rows), jnp.float32),
        pltpu.VMEM((rows, rows), jnp.float32),
        pltpu.VMEM((HEAD_SIZE + ONES_ROWS, rows), jnp.bfloat16),
        pltpu.VMEM((HEAD_SIZE + ONES_ROWS, rows), jnp.bfloat16),
    ]


def params_of(heads, rows, blocks, limit=VMEM_LIMIT):
    return dict(
        compiler_params=pltpu.CompilerParams(vmem_limit_bytes=limit),
        cost_estimate=pl.CostEstimate(
            flops=int(heads * rows * HEAD_SIZE * blocks),
            bytes_accessed=heads * rows,
            transcendentals=0,
        ),
    )


def state_shapes(group, rows):
    span = group * HEAD_SIZE
    stats = jax.ShapeDtypeStruct((2, group, rows), jnp.float32)
    return [
        jax.ShapeDtypeStruct((2, span, rows), jnp.bfloat16),
        stats,
        jax.ShapeDtypeStruct((2, span, rows), jnp.float32),
        stats,
        stats,
    ]


def own_attention(flags, queries, keys, values, group, kv_heads, shared):
    rows = queries.shape[0]
    span = group * HEAD_SIZE
    states = pl.pallas_call(
        functools.partial(own_kernel, kv_heads, shared),
        in_specs=[SMEM, HBM, HBM, HBM],
        out_specs=[VMEM] * (5 * kv_heads),
        out_shape=state_shapes(group, rows) * kv_heads,
        scratch_shapes=[
            pltpu.VMEM((kv_heads, rows, span), jnp.bfloat16),
            pltpu.SemaphoreType.DMA((3 * kv_heads,)),
            pltpu.VMEM((kv_heads, rows, 2 * HEAD_SIZE), jnp.bfloat16),
            *scratch_of(rows),
        ],
        name="attend_own",
        **params_of(kv_heads * group, rows, 1, OWN_VMEM_LIMIT),
    )(flags, queries, keys, values)
    return [states[5 * h:5 * h + 5] for h in range(kv_heads)]


def chip_pairs(flags, keys, values, got, kv_heads, shared):
    rows = keys.shape[0]
    *pairs, span = pl.pallas_call(
        functools.partial(pair_kernel, kv_heads, shared),
        in_specs=[SMEM, VMEM, VMEM, VMEM],
        out_specs=[VMEM] * kv_heads + [SMEM],
        out_shape=[jax.ShapeDtypeStruct((2, rows, 2 * HEAD_SIZE), jnp.bfloat16)] * kv_heads
        + [jax.ShapeDtypeStruct((1,), jnp.int32)],
        compiler_params=pltpu.CompilerParams(vmem_limit_bytes=8 * MIB),
        name="chip_pairs",
    )(flags, keys, values, got)
    return pairs, span[0]


def phase(jobs, flags, received, kvs, states, placed, width, group, kv_heads):
    rows = states[0][0].shape[2]
    span = group * HEAD_SIZE
    ends, opens = jobs[0][1] == BEYOND, jobs[-1][1] == OTHER
    args, in_specs = [flags], [SMEM]
    if opens:
        args, in_specs = args + [received], in_specs + [VMEM]
    out_shape, out_specs, aliases, where = [], [], {}, []
    for (h, stage), kv in zip(jobs, kvs):
        for at in WRITTEN[stage]:
            aliases[len(args) + 1 + at] = len(out_shape)
            where.append((h, at))
            out_shape.append(state_shapes(group, rows)[at])
            out_specs.append(VMEM)
        args += [kv, *states[h]]
        in_specs += [VMEM] * 6
    scratch = scratch_of(rows)
    if ends:
        if placed is not None:
            aliases[len(args)] = len(out_shape)
            args, in_specs = args + [placed], in_specs + [HBM]
        out_shape += [
            jax.ShapeDtypeStruct((rows, width), jnp.bfloat16),
            jax.ShapeDtypeStruct((rows, span), jnp.bfloat16),
        ]
        out_specs += [HBM, HBM]
        scratch = [
            pltpu.VMEM((2, rows, span), jnp.bfloat16),
            pltpu.SemaphoreType.DMA((2,)),
            *scratch,
        ]
    results = pl.pallas_call(
        functools.partial(phase_kernel, jobs, kv_heads, int(placed is not None and ends)),
        in_specs=in_specs,
        out_specs=out_specs,
        out_shape=out_shape,
        scratch_shapes=scratch,
        input_output_aliases=aliases,
        name="attend" + "".join(f"_{'other second first beyond'.split()[k]}{h}" for h, k in jobs),
        **params_of(2 * group, rows, 1),
    )(*args)
    for (h, at), result in zip(where, results):
        states[h][at] = result
    return results[len(where):]


def cut_out(flags, queries):
    rows, width = queries.shape
    return pl.pallas_call(
        cut_kernel,
        in_specs=[SMEM, HBM],
        out_specs=VMEM,
        out_shape=jax.ShapeDtypeStruct((rows, width // 2), queries.dtype),
        scratch_shapes=[pltpu.SemaphoreType.DMA((1,))],
        compiler_params=pltpu.CompilerParams(vmem_limit_bytes=CUT_VMEM_LIMIT),
        name="cut_queries",
    )(flags, queries)


def put_in(flags, pieces, out):
    return pl.pallas_call(
        place_kernel,
        in_specs=[SMEM] + [VMEM] * len(pieces) + [HBM],
        out_specs=HBM,
        out_shape=jax.ShapeDtypeStruct(out.shape, out.dtype),
        scratch_shapes=[pltpu.SemaphoreType.DMA((len(pieces),))],
        input_output_aliases={1 + len(pieces): 0},
        compiler_params=pltpu.CompilerParams(vmem_limit_bytes=4 * MIB),
        name="place_result",
    )(flags, *pieces, out)


def on_device(queries, keys, values, prefix_spans):
    rows, width = queries.shape
    length = lax.axis_size("ctx")
    kv_local = keys.shape[1] // HEAD_SIZE
    shared = kv_local % 2 == 1
    kv_heads, group = (kv_local, GROUP // 2) if shared else (kv_local // 2, GROUP)
    q_width, kv_width = width // 2, kv_heads * HEAD_SIZE

    position = lax.axis_index("ctx")
    core = position % 2
    lower = (position // 2) % 2 == 0
    swap = [(i, i ^ 1) for i in range(length)]
    across = [(i, i ^ 2) for i in range(length)]
    ahead = [(i, i + 4) for i in range(length - 4)]

    def theirs(a):
        return a if shared else jnp.where(core == 0, a[:, kv_width:], a[:, :kv_width])

    span_columns = jnp.broadcast_to(prefix_spans.astype(jnp.bfloat16), (rows, HEAD_SIZE))
    core_flag = core[None].astype(jnp.int32)
    kv_sent = jnp.concatenate([theirs(keys), theirs(values), span_columns], axis=1)
    kv_got, cut_flag = lax.optimization_barrier((moved(kv_sent, swap), core_flag))
    q_got = moved(cut_out(cut_flag, queries), swap)
    pairs, other_span = chip_pairs(core_flag, keys, values, kv_got, kv_heads, shared)

    reach_own = jnp.minimum(prefix_spans[0], position)
    reach_other = jnp.minimum(other_span, position ^ 1)

    def counts(distance):
        first = 2 * distance - 1
        return [
            jnp.clip(reach_own - first - core + 1, 0, 2),
            jnp.clip(reach_other - first - (1 - core) + 1, 0, 2),
        ]

    flags = jnp.stack([core, *[n for d in range(1, 5) for n in counts(d)]]).astype(jnp.int32)

    def across_of(pair, second):
        return moved(jnp.where(lower, pair, second), across)

    heads = range(kv_heads)
    second = [moved(pairs[h], ahead) for h in heads]
    states = own_attention(core_flag, queries, keys, values, group, kv_heads, shared)
    states = [list(state) for state in states]
    first, beyond, out, returned = {}, {}, None, []
    for t in range(kv_heads + 3):
        jobs = [(h, t - h) for h in heads if 0 <= t - h <= BEYOND]
        arrived = [[pairs, second, first, beyond][stage][h] for h, stage in jobs]
        if t > 0:
            arrived, states = lax.optimization_barrier((arrived, states))
        for (h, stage), kv in zip(jobs, arrived):
            if stage == SECOND:
                second[h] = kv
                first[h] = across_of(pairs[h], kv)
            if stage == FIRST:
                beyond[h] = moved(jnp.concatenate([kv, second[h][:1]]), ahead)
        done = phase(jobs, flags, q_got, arrived, states, out, width, group, kv_heads)
        if done:
            out = done[0]
            returned.append(moved(done[1], swap))
    return put_in(core_flag, returned, out)


def solution(mesh):
    placed = (P("ctx", "tp"), P("ctx", "tp"), P("ctx", "tp"), P("ctx"))
    return jax.shard_map(
        on_device, mesh=mesh, in_specs=placed, out_specs=P("ctx", "tp"), check_vma=False
    )
```
